512 devices in a mesh: band: 4 (over x), tm: 128 (over y, z, core).
Axes of the slice: x: 4, y: 8, z: 8, core: 2. Of those that a mesh axis runs over, the one named last changes fastest.
Arguments:
- timeline: bfloat16 [65536, 1024], P('tm', 'band'), parts along dimension 1, may hold values from -6 to 6
- pointing: int32 [65536, 1024], P('tm', 'band'), parts along dimension 1, may hold values from 0 to 127
- plate_angle: float32 [65536], P('tm'), may hold values from -3.140625 to 3.140625
- detector_angle: float32 [1024], P('band'), parts along dimension 0, may hold values from -3.140625 to 3.140625
- detector_weight: float32 [1024], P('band'), parts along dimension 0, may hold values from 0.3 to 3
- kernel: bfloat16 [4100], P('band'), parts along dimension 0, may hold values from -0.1875 to 0.1875
- tile_owner: int32 [8192, 4], P('tm', 'band'), parts along dimension 1, may hold values from 0 to 127; in each aligned block of 64 rows (0 to 63, 64 to 127, ...) at most 2 rows name the same one
- tile_block: int32 [8192, 4], P('tm', 'band'), parts along dimension 1, may hold values from 0 to 511
- wiener: float32 [12, 4096, 2048], P('band', 'tm'), parts along dimension 0, may hold values from 0.05 to 1
Outputs:
- filtered_spectrum: float32 [2, 12, 4096, 2048], P(None, 'band', 'tm'), parts along dimension 1
The draws below stay inside these ranges and needn't reach their ends.
There are 4 independent parts, one for each index of `band`. The reference program is written for one: setup_inputs(seed, part) draws one part's arguments, and reference() takes and returns one part's arrays. A program takes and returns all parts, laid end to end along the dimension named above; an argument that names none is the same for every part. Nothing has to cross between parts.
Inputs may be any that keep to these rules, and one draw needn't show every extreme that they name: `tile_owner`: at most 2 of the 64 tiles of one time shard name the same owner, some shard's tiles name one owner exactly 2 times, and every owner is named by some tile.
All inputs are finite; a program needn't handle non-finite values.
Results may differ from the reference program's by a relative error of at most 0.0029.
Values may be sent and summed in bfloat16 or wider, within the bound.
A program may use at most 128 MiB of HBM per device.

```python
import math
import jax
import jax.numpy as jnp
import numpy as np
from jax import lax

DET = 256
HALF = 512
PIECE = 16
DGRP = 128
BPIX = 128
ROWS = 2048
COLS = 4096
SAMPLES = 65536
KLEN = 1025
NTILE = 64
TILES = 8192
CAP = 2
ROWS_OWN = 16
COL_BLOCKS = 32
OWNBLK = 512
N_TM = 128


def set_ends(entries, own_key, least, largest):
    longest = entries.shape.index(max(entries.shape))
    spots = []
    for shift in (0, 1):
        where = [jax.random.randint(jax.random.fold_in(own_key, axis), (), 0, length) for axis, length in enumerate(entries.shape)]
        where[longest] = (where[longest] + shift) % entries.shape[longest]
        spots.append(tuple(where))
    return entries.at[spots[0]].set(least).at[spots[1]].set(largest)


def block_levels(rng, dims, split, least, top_value):
    level = 1.0
    for position, blocks in split:
        draws = jax.random.uniform(jax.random.fold_in(jax.random.fold_in(rng, 6), position), (blocks,), jnp.float32, least / len(split), top_value / len(split))
        level = level * jnp.repeat(jnp.exp(draws), dims[position] // blocks).reshape((-1,) + (1,) * (len(dims) - 1 - position))
    return level


def routed_block(stream_key, own, number, rows, count, top, reach, lean):
    sequence = jax.random.permutation(stream_key, count)
    crowded, ordinary = shares(count, rows * top, reach, lean, True), shares(count, rows * top, reach, lean, False)
    places = jnp.arange(count)

    def named(lengths, offset_by):
        used = int((lengths > 0).sum())
        fixed = max(1, used // 4)
        passed = fixed + (places - fixed + offset_by * (used - fixed)) % max(1, count - fixed)
        return jnp.zeros((count,), jnp.int32).at[sequence[jnp.where(places < fixed, places, passed)]].set(jnp.asarray(lengths, jnp.int32))

    lengths = jnp.where(number % 4 == 0, named(crowded, number // 4), named(ordinary, number - number // 4 - 1))
    mixed = jax.random.permutation(jax.random.fold_in(own, 3), count)
    donor, taker = mixed[0:count // 2 * 2:2], mixed[1:count // 2 * 2:2]
    room = jnp.minimum(lengths[donor] - 1, reach - lengths[taker]) // 2
    room = jnp.where((donor == sequence[0]) | (taker == sequence[0]) | (lengths[taker] == 0), 0, jnp.maximum(room, 0))
    passed = jax.random.randint(jax.random.fold_in(own, 4), (count // 2,), 0, 1 << 20) % (room + 1)
    lengths = lengths.at[donor].add(-passed).at[taker].add(passed)
    items = jnp.searchsorted(jnp.cumsum(lengths), jnp.arange(rows * top), side="right").astype(jnp.int32)
    grid = items.reshape(top, rows).T
    grid = grid[jax.random.permutation(jax.random.fold_in(own, 1), rows)]
    offset_by = jax.random.randint(jax.random.fold_in(own, 2), (rows, 1), 0, top)
    return jnp.take_along_axis(grid, (jnp.arange(top)[None, :] + offset_by) % top, axis=1)


def shares(count, total, reach, slope, full):
    weights = [(1 << 20) // math.isqrt(standing ** slope) + 1 for standing in range(1, count + 1)]
    largest = reach if full else min(reach, max(-(-total // count), total * weights[0] // sum(weights)))
    least = 1 if total - largest >= count - 1 else 0
    holding, surplus = [largest] + [least] * (count - 1), total - largest - least * (count - 1)
    while surplus > 0:
        free = [i for i in range(1, count) if holding[i] < largest] or [i for i in range(1, count) if holding[i] < reach]
        whole, budget = sum([weights[i] for i in free]), surplus
        for i in free:
            addition = min(reach - holding[i], max(1, budget * weights[i] // whole), surplus)
            holding[i] = holding[i] + addition
            surplus = surplus - addition
    return np.array(holding)


def scatter_about(key, dims, width, most, pieces=(), kind=jnp.bfloat16):
    entries = width * jax.random.normal(key, dims, jnp.float32)
    if pieces:
        entries = entries * block_levels(key, dims, pieces, -0.22, 0.18)
    return jnp.clip(entries, -most, most).astype(kind)


def setup_inputs(seed: int = 0, part: int = 0) -> dict:
    key_list = jax.random.split(jax.random.key(seed), 10)
    part_keys = jax.random.split(jax.random.fold_in(key_list[9], part), 10)
    timeline = scatter_about(part_keys[0], (SAMPLES, DET), 1.0, 6.0, ((0, 128),))
    pointing = set_ends(jax.random.randint(part_keys[1], (SAMPLES, DET), 0, BPIX), jax.random.fold_in(part_keys[1], 1), 0, BPIX - 1).astype(jnp.int32)
    plate_angle = jnp.clip(jax.random.uniform(key_list[2], (SAMPLES,), jnp.float32, -3.140625, 3.140625), -3.140625, 3.140625)
    detector_angle = jnp.clip(jax.random.uniform(part_keys[3], (DET,), jnp.float32, -3.140625, 3.140625), -3.140625, 3.140625)
    detector_weight = jnp.clip(jnp.exp(jax.random.uniform(part_keys[4], (DET,), jnp.float32, math.log(0.3), math.log(3.0))), 0.3, 3.0)
    kernel = scatter_about(part_keys[5], (KLEN,), KLEN ** -0.5, 0.1875)
    tile_owner_keys = jax.random.split(jax.random.fold_in(part_keys[6], 1), TILES // NTILE)
    tile_owner_turns = jax.random.permutation(jax.random.fold_in(part_keys[6], 3), TILES // NTILE)
    tile_owner = jax.vmap(lambda own, number: routed_block(jax.random.fold_in(part_keys[6], 2), own, number, NTILE, N_TM, 1, CAP, 2))(tile_owner_keys, tile_owner_turns).reshape((TILES, 1))
    tile_block = set_ends(jax.random.randint(part_keys[7], (TILES, 1), 0, OWNBLK), jax.random.fold_in(part_keys[7], 1), 0, OWNBLK - 1).astype(jnp.int32)
    wiener = jnp.clip(0.05 + 0.95 * jax.random.uniform(part_keys[8], (3, COLS, ROWS), jnp.float32) ** block_levels(part_keys[8], (3, COLS, ROWS), ((1, 128),), -0.2, 0.2), 0.05, 1.0)
    return {"timeline": timeline, "pointing": pointing, "plate_angle": plate_angle, "detector_angle": detector_angle, "detector_weight": detector_weight, "kernel": kernel, "tile_owner": tile_owner, "tile_block": tile_block, "wiener": wiener}


def band_matrix(kernel):
    half_width = (kernel.shape[0] - 1) // 2
    pattern = jnp.concatenate([kernel, jnp.zeros((half_width,), kernel.dtype)])
    repeated = jnp.tile(pattern, half_width)[: 3 * half_width * half_width]
    return repeated.reshape(half_width, 3 * half_width)


def apply_band(padded, band_rows):
    half_width = band_rows.shape[0]
    blocks = padded.reshape(-1, half_width, padded.shape[1])
    windows = jnp.concatenate([blocks[:-2], blocks[1:-1], blocks[2:]], axis=1)
    result = jnp.einsum("ij,bjc->bic", band_rows.astype(jnp.float32), windows.astype(jnp.float32), precision=lax.Precision.HIGHEST)
    return result.reshape(-1, padded.shape[1])


def reference(timeline, pointing, plate_angle, detector_angle, detector_weight, kernel, tile_owner, tile_block, wiener):
    band_rows = band_matrix(kernel)
    padded = jnp.pad(timeline, ((HALF, HALF), (0, 0)))
    weighted = detector_weight[None, :] * apply_band(padded, band_rows)
    angle = 2.0 * plate_angle[:, None] + detector_angle[None, :]
    stokes = jnp.stack([weighted, weighted * jnp.cos(2.0 * angle), weighted * jnp.sin(2.0 * angle)]).astype(jnp.bfloat16)
    sample_tile = (jnp.arange(SAMPLES, dtype=jnp.int32) // PIECE)[:, None] * (DET // DGRP) + (jnp.arange(DET, dtype=jnp.int32) // DGRP)[None, :]
    owners = tile_owner[:, 0][sample_tile]
    blocks = tile_block[:, 0][sample_tile]
    map_row = owners * ROWS_OWN + blocks // COL_BLOCKS
    map_col = (blocks % COL_BLOCKS) * BPIX + pointing
    flat = (map_row * COLS + map_col).reshape(-1).astype(jnp.int32)
    sums = jax.ops.segment_sum(stokes.reshape(3, -1).T.astype(jnp.float32), flat, num_segments=ROWS * COLS)
    sky = sums.T.reshape(3, ROWS, COLS)
    spectrum = jnp.fft.fft2(sky, norm="ortho")
    real_part = jnp.real(spectrum).astype(jnp.float32)
    imag_part = jnp.imag(spectrum).astype(jnp.float32)
    stacked = jnp.stack([real_part, imag_part]).transpose(0, 1, 3, 2)
    return stacked * wiener[None]
```

```python
import functools
import math

import jax
import jax.numpy as jnp
import numpy as np
from jax import lax
from jax.experimental import pallas as pl
from jax.experimental.pallas import tpu as pltpu
from jax.sharding import PartitionSpec as P

DET = 256
TS = 512
PIECE = 16
DGRP = 128
BPIX = 128
ROWS = 2048
COLS = 4096
NTILE = 64
N_TM = 128
SIDE = 8
TAPS_PAD = 1280
MESH = pl.DeviceIdType.MESH
F32 = jnp.float32
BF16 = jnp.bfloat16


def ring_dist(d):
    return min(d, SIDE - d)


def dot(a, b, dims=((1,), (0,))):
    return lax.dot_general(a, b, (dims, ((), ())), preferred_element_type=F32)


def iota(shape, axis):
    return lax.broadcasted_iota(jnp.int32, shape, axis)


def map_kernel(
    timeline, pointing, plate, det_angle, det_weight, taps, owner, block,
    rows_out,
    window, toep, trig, vals, pixels, spread, low_hot, local, gathered, meta, basis, turn,
    halo_send, halo_recv, m1_send, m1_recv, m2_send, m2_recv,
    p1_send, p1_recv, p2_send, p2_recv, sib_send, sib_recv,
):
    band = lax.axis_index("band")
    me = lax.axis_index("tm")
    y = me // 16
    z = (me // 2) % SIDE
    c = me % 2
    zc = me % 16

    def dev(yy, zz, cc):
        return (band, (yy % SIDE) * 16 + (zz % SIDE) * 2 + cc)

    right, left = (band, (me + 1) % N_TM), (band, (me + N_TM - 1) % N_TM)
    plane = [(band, y * 16 + (zc + k) % 16) for k in range(1, 16)]
    column = [dev(y + k, z, c) for k in range(1, SIDE)]
    barrier = pltpu.get_barrier_semaphore()
    for other in plane + column + [right, left]:
        pl.semaphore_signal(barrier, inc=1, device_id=other, device_id_type=MESH)

    lane = iota((NTILE, 128), 1)
    q, a = (lane % NTILE) // 8, lane % 8
    wanted = ((q // 2) * 8 + a) * 2 + q % 2
    place = jnp.where((lane // NTILE == c) & (wanted == iota((NTILE, 128), 0)), 1.0, 0.0)
    sub = iota((8, NTILE), 0)
    parts = jnp.where(
        sub == 0, owner[...], jnp.where(sub == 1, block[...] // 32, block[...] % 32)
    ).astype(F32)
    spots = dot(parts.astype(BF16), place.astype(BF16)).astype(jnp.int32)
    meta[y, zc] = (spots[0:1] * 16 + spots[1:2]) * 32 + spots[2:3]

    pl.semaphore_wait(barrier, 24)

    def remote(src, dst, send, recv, to):
        copy = pltpu.make_async_remote_copy(
            src_ref=src, dst_ref=dst, send_sem=send, recv_sem=recv, device_id=to, device_id_type=MESH
        )
        copy.start()
        return copy

    pending = []
    halo = [
        remote(timeline, window.at[pl.ds(0, TS)], halo_send.at[0], halo_recv.at[0], right),
        remote(timeline, window.at[pl.ds(2 * TS, TS)], halo_send.at[1], halo_recv.at[1], left),
    ]
    first_meta = [
        remote(meta.at[y, zc], meta.at[y, zc], m1_send.at[k], m1_recv.at[k], to)
        for k, to in enumerate(plane)
    ]

    window[TS : 2 * TS, :] = timeline[...]
    band_rows = jnp.broadcast_to(taps[...], (256, TAPS_PAD))
    toep[...] = pltpu.roll(band_rows, 0, 1, stride=1, stride_axis=0).astype(BF16)
    for half in range(2):
        pixels[half] = pointing[:, half * 128 : half * 128 + 128]
    for part in range(4):
        turned = jnp.transpose(jnp.broadcast_to(plate[part : part + 1, :], (128, 128)))
        for half in range(2):
            lanes = slice(half * 128, half * 128 + 128)
            angle = 2.0 * turned + det_angle[:, lanes]
            trig[0, part * 128 : part * 128 + 128, lanes] = jnp.cos(2.0 * angle)
            trig[1, part * 128 : part * 128 + 128, lanes] = jnp.sin(2.0 * angle)
    row = iota((BPIX, 128), 0)
    lane = iota((BPIX, 128), 1)
    pixel = (row % 8) * 16 + row // 8
    step = (((me * 32 + lane % 32) * pixel) % COLS).astype(F32) * (2.0 * math.pi / COLS)
    cos_x, sin_x = jnp.cos(step), jnp.sin(step)
    for s in range(3):
        mine = lane // 32 == s
        whole = jnp.concatenate([jnp.where(mine, cos_x, 0.0), jnp.where(mine, -sin_x, 0.0)], axis=1)
        high = whole.astype(BF16)
        basis[s * 128 : s * 128 + 128, :] = high
        basis[384 + s * 128 : 384 + s * 128 + 128, :] = (whole - high.astype(F32)).astype(BF16)
    step = ((iota((32, 128), 0) * (iota((32, 128), 1) % 32)) % 32).astype(F32) * (2.0 * math.pi / 32)
    whole = jnp.concatenate([jnp.cos(step), jnp.sin(step)], axis=1)
    high = whole.astype(BF16)
    turn[0:32, :] = high
    turn[32:64, :] = (whole - high.astype(F32)).astype(BF16)
    rows_out[...] = jnp.zeros_like(rows_out)

    for copy in first_meta:
        copy.wait_recv()
    second_meta = [
        remote(meta.at[y], meta.at[y], m2_send.at[k], m2_recv.at[k], to)
        for k, to in enumerate(column)
    ]
    for copy in halo:
        copy.wait_recv()

    @pl.when(me == 0)
    def _():
        window[0:TS, :] = jnp.zeros((TS, DET), BF16)

    @pl.when(me == N_TM - 1)
    def _():
        window[2 * TS : 3 * TS, :] = jnp.zeros((TS, DET), BF16)

    for part in range(2):
        rows = slice(part * 256, part * 256 + 256)
        filtered = dot(toep[...], window[part * 256 : part * 256 + TAPS_PAD, :])
        weighted = det_weight[...] * filtered
        for half in range(2):
            lanes = slice(half * 128, half * 128 + 128)
            vals[half, rows, :] = weighted[:, lanes]
            vals[2 + half, rows, :] = weighted[:, lanes] * trig[0, rows, lanes]
            vals[4 + half, rows, :] = weighted[:, lanes] * trig[1, rows, lanes]

    lane = iota((8, 128), 1)
    pick = (lane // 8) * 8 + iota((8, 128), 0)

    def bin_tiles(q, carry):
        first = (q // 2) * 128
        for t in range(PIECE):
            where = pl.ds(first + t, 8, stride=PIECE)
            pixel = pixels[q % 2, where, :]
            high, low = pixel // 16, pixel % 16
            value = [vals[2 * s + q % 2, where, :] for s in range(3)]
            at = slice(t * 128, t * 128 + 128)
            for pair in range(12):
                both = []
                for k in (2 * pair, 2 * pair + 1):
                    both.append(jnp.where(high == k // 3, value[k % 3], 0.0))
                spread[pair * 16 : pair * 16 + 16, at] = jnp.concatenate(both, axis=0).astype(BF16)
            for pair in range(8):
                both = [jnp.where(low == k, 1.0, 0.0) for k in (2 * pair, 2 * pair + 1)]
                low_hot[pair * 16 : pair * 16 + 16, at] = jnp.concatenate(both, axis=0).astype(BF16)
        crossed = dot(spread[...], low_hot[...], ((1,), (1,)))
        for s in range(3):
            total = jnp.zeros((8, 128), F32)
            for h in range(8):
                k = h * 3 + s
                own = jnp.take_along_axis(crossed[k * 8 : k * 8 + 8], pick, axis=1)
                total = jnp.where(lane % 8 == h, own, total)
            local[pl.ds(pl.multiple_of(q * 8, 8), 8), s * 128 : s * 128 + 128] = total
        return carry

    lax.fori_loop(0, 8, bin_tiles, 0)

    for copy in second_meta:
        copy.wait_recv()
    pending += halo + first_meta + second_meta

    c1, c0 = c, 1 - c
    up = dev(y + c0, z + c1, c)
    down = dev(y + SIDE - c0, z + SIDE - c1, c)
    peers = [dev(y + c1 * k, z + c0 * k, c) for k in range(1, SIDE)]
    sibling = dev(y, z, 1 - c)

    def chip(d2, d1):
        return ((y + 16 - c1 * d1 - c0 * d2) % SIDE) * SIDE + (z + 16 - c0 * d1 - c1 * d2) % SIDE

    half = pl.ds(pl.multiple_of(c * NTILE, NTILE), NTILE)
    gathered[y * SIDE + z, half] = local[...].astype(BF16)

    def forward(d2, d1, send, recv, to):
        piece = gathered.at[chip(d2, d1), half]
        return remote(piece, piece, send, recv, to)

    arriving = {}
    siblings = {}
    order = sorted(
        (ring_dist(d2) + ring_dist(d1) / 4, ring_dist(d1), d2, d1)
        for d2 in range(SIDE)
        for d1 in range(SIDE)
    )

    def along_second(d2, d1):
        k = d2 + 1
        if d2 < 3 or (d2 == 3 and d1 < 4):
            arriving[k, d1] = forward(d2, d1, p2_send.at[k * 8 + d1], p2_recv.at[k * 8 + d1], up)
        k = (d2 + 7) % SIDE
        if d2 in (0, 6, 7) or (d2 == 5 and d1 >= 4):
            arriving[k, d1] = forward(d2, d1, p2_send.at[k * 8 + d1], p2_recv.at[k * 8 + d1], down)

    key_rows = iota((256, 512), 0)
    turn_rows = iota((64, 512), 0) % 32

    def use(chips):
        tiles = jnp.concatenate([gathered[i] for i in chips], axis=0)
        codes = jnp.concatenate(
            [meta[i // SIDE, (i % SIDE) * 2] + meta[i // SIDE, (i % SIDE) * 2 + 1] for i in chips],
            axis=1,
        )
        spectra = dot(tiles, basis[0:384]) + dot(tiles, basis[384:768])
        turn_hot = jnp.where(turn_rows == codes % 32, 1.0, 0.0).astype(BF16)
        turned = dot(turn_hot, turn[...], ((0,), (0,)))
        real, imag = spectra[:, 0:128], spectra[:, 128:256]
        cos_b, sin_b = turned[:, 0:128], turned[:, 128:256]
        moved = jnp.concatenate(
            [real * cos_b + imag * sin_b, imag * cos_b - real * sin_b], axis=1
        ).astype(BF16)
        map_row = codes // 32
        low, high = map_row % 8, map_row // 8

        def add(r, carry):
            key = jnp.where(low == r, high, -1)
            hot = jnp.where(key_rows == key, 1.0, 0.0).astype(BF16)
            at = pl.ds(pl.multiple_of(r * 256, 256), 256)
            rows_out[at, :] += dot(hot, moved)
            return carry

        lax.fori_loop(0, 8, add, 0)

    turn_at = {(e[2], e[3]): n for n, e in enumerate(order)}
    ready = sorted((max(turn_at[i, j], turn_at[j, i]), i, j) for i, j in turn_at)
    used = 0

    def use_ready(reached):
        nonlocal used
        while used < len(ready) and ready[used + 3][0] <= reached:
            group = [(i, j) for _, i, j in ready[used : used + 4]]
            used += 4
            for i, j in group:
                siblings[j, i].wait_recv()
            use([chip(i, j) for i, j in group])

    lag = 6
    for n, (_, _, d2, d1) in enumerate(order):
        if n:
            arriving[d2, d1].wait_recv()
        along_second(d2, d1)
        if n == 0:
            for k in (1, 7, 2, 6, 3, 5, 4):
                arriving[0, k] = forward(0, 0, p1_send.at[k], p1_recv.at[k], peers[k - 1])
        siblings[d2, d1] = forward(
            d2, d1, sib_send.at[d2 * 8 + d1], sib_recv.at[d2 * 8 + d1], sibling
        )
        use_ready(n - lag)
    use_ready(len(order))
    pending += list(arriving.values()) + list(siblings.values())
    for copy in pending:
        copy.wait_send()


def eighth(parts):
    def add(u, v):
        return (u[0] + v[0], u[1] + v[1])

    def sub(u, v):
        return (u[0] - v[0], u[1] - v[1])

    def turn(u):
        return (u[1], -u[0])

    def four(u):
        s, d, t, e = add(u[0], u[2]), sub(u[0], u[2]), add(u[1], u[3]), turn(sub(u[1], u[3]))
        return [add(s, t), add(d, e), sub(s, t), sub(d, e)]

    even, odd = four(parts[0::2]), four(parts[1::2])
    h = math.sqrt(0.5)
    odd[1] = ((odd[1][0] + odd[1][1]) * h, (odd[1][1] - odd[1][0]) * h)
    odd[2] = turn(odd[2])
    odd[3] = ((odd[3][1] - odd[3][0]) * h, (-odd[3][0] - odd[3][1]) * h)
    return [add(even[k], odd[k]) for k in range(4)] + [sub(even[k], odd[k]) for k in range(4)]


def column_kernel(rows, high, low, wiener, out):
    lines = []
    for r in range(8):
        at = slice(r * 256, r * 256 + 256)
        both = jnp.concatenate(
            [jnp.transpose(rows[at, 0:128])[0:96], jnp.transpose(rows[at, 128:256])[0:96]], axis=0
        )
        upper = both.astype(BF16)
        stacked = jnp.concatenate([upper, (both - upper.astype(F32)).astype(BF16)], axis=0)
        waves = []
        for w in range(2):
            wide = dot(stacked, high[r, w])
            waves.append(wide[0:192] + wide[192:384] + dot(upper, low[r, w]))
        lines.append((waves[0][0:96] + waves[1][96:192], waves[0][96:192] - waves[1][0:96]))
    scale = 1.0 / math.sqrt(ROWS * COLS)
    for k, (real, imag) in enumerate(eighth(lines)):
        at = slice(k * 256, k * 256 + 256)
        for s in range(3):
            gain = wiener[s, :, at] * scale
            out[0, s, :, at] = real[s * 32 : s * 32 + 32] * gain
            out[1, s, :, at] = imag[s * 32 : s * 32 + 32] * gain


def column_tables():
    r0 = np.arange(256)[None, :, None]
    r1 = np.arange(8)[:, None, None]
    k = np.arange(256)[None, None, :]
    phase = (k * (r1 + 8 * r0) % ROWS) * (2.0 * np.pi / ROWS)
    table = np.stack([np.cos(phase), np.sin(phase)], axis=1)
    high = table.astype(BF16)
    low = (table - high.astype(np.float64)).astype(BF16)
    return high, low


def owned_rows(timeline, pointing, plate_angle, detector_angle, detector_weight, kernel, tile_owner, tile_block):
    taps = jnp.pad(kernel.astype(F32), (0, TAPS_PAD - kernel.shape[0])).reshape(1, TAPS_PAD)
    vmem = pl.BlockSpec(memory_space=pltpu.VMEM)
    dma = pltpu.SemaphoreType.DMA
    return pl.pallas_call(
        map_kernel,
        out_shape=jax.ShapeDtypeStruct((ROWS, 256), F32),
        in_specs=[vmem] * 8,
        out_specs=vmem,
        scratch_shapes=[
            pltpu.VMEM((3 * TS, DET), BF16),
            pltpu.VMEM((256, TAPS_PAD), BF16),
            pltpu.VMEM((2, TS, DET), F32),
            pltpu.VMEM((6, TS, 128), F32),
            pltpu.VMEM((2, TS, 128), jnp.int32),
            pltpu.VMEM((192, PIECE * DGRP), BF16),
            pltpu.VMEM((128, PIECE * DGRP), BF16),
            pltpu.VMEM((NTILE, 384), F32),
            pltpu.VMEM((64, 2 * NTILE, 384), BF16),
            pltpu.VMEM((8, 16, 1, 128), jnp.int32),
            pltpu.VMEM((768, 256), BF16),
            pltpu.VMEM((64, 256), BF16),
            dma((2,)), dma((2,)), dma((15,)), dma((15,)), dma((7,)), dma((7,)),
            dma((8,)), dma((8,)), dma((64,)), dma((64,)), dma((64,)), dma((64,)),
        ],
        compiler_params=pltpu.CompilerParams(
            collective_id=0, has_side_effects=True, vmem_limit_bytes=48 << 20
        ),
        cost_estimate=pl.CostEstimate(flops=20 << 30, bytes_accessed=4 << 20, transcendentals=1 << 20),
    )(
        timeline,
        pointing,
        plate_angle.reshape(4, 128),
        detector_angle.reshape(1, DET),
        detector_weight.reshape(1, DET),
        taps,
        tile_owner.reshape(1, NTILE),
        tile_block.reshape(1, NTILE),
    )


def columns(rows, wiener):
    vmem = pl.BlockSpec(memory_space=pltpu.VMEM)
    high, low = column_tables()
    return pl.pallas_call(
        column_kernel,
        out_shape=jax.ShapeDtypeStruct((2, 3, 32, ROWS), F32),
        in_specs=[vmem] * 4,
        out_specs=vmem,
        compiler_params=pltpu.CompilerParams(vmem_limit_bytes=48 << 20),
        cost_estimate=pl.CostEstimate(flops=4 << 30, bytes_accessed=9 << 20, transcendentals=0),
    )(rows, jnp.asarray(high), jnp.asarray(low), wiener)


def body(*arrays):
    return columns(owned_rows(*arrays[:8]), arrays[8])


def solution(mesh):
    placed = (
        P("tm", "band"),
        P("tm", "band"),
        P("tm"),
        P("band"),
        P("band"),
        P("band"),
        P("tm", "band"),
        P("tm", "band"),
        P("band", "tm", None),
    )
    return jax.shard_map(
        body, mesh=mesh, in_specs=placed, out_specs=P(None, "band", "tm", None), check_vma=False
    )
```

```python
import functools
import math

import jax
import jax.numpy as jnp
import numpy as np
from jax import lax
from jax.experimental import pallas as pl
from jax.experimental.pallas import tpu as pltpu
from jax.sharding import PartitionSpec as P

DET = 256
TS = 512
PIECE = 16
DGRP = 128
BPIX = 128
ROWS = 2048
COLS = 4096
NTILE = 64
N_TM = 128
SIDE = 8
TAPS_PAD = 1280
MESH = pl.DeviceIdType.MESH
F32 = jnp.float32
BF16 = jnp.bfloat16


def dot(a, b, dims=((1,), (0,))):
    return lax.dot_general(a, b, (dims, ((), ())), preferred_element_type=F32)


def iota(shape, axis):
    return lax.broadcasted_iota(jnp.int32, shape, axis)


def eighth(parts):
    def add(u, v):
        return (u[0] + v[0], u[1] + v[1])

    def sub(u, v):
        return (u[0] - v[0], u[1] - v[1])

    def turn(u):
        return (u[1], -u[0])

    def four(u):
        s, d, t, e = add(u[0], u[2]), sub(u[0], u[2]), add(u[1], u[3]), turn(sub(u[1], u[3]))
        return [add(s, t), add(d, e), sub(s, t), sub(d, e)]

    even, odd = four(parts[0::2]), four(parts[1::2])
    h = math.sqrt(0.5)
    odd[1] = ((odd[1][0] + odd[1][1]) * h, (odd[1][1] - odd[1][0]) * h)
    odd[2] = turn(odd[2])
    odd[3] = ((odd[3][1] - odd[3][0]) * h, (-odd[3][0] - odd[3][1]) * h)
    return [add(even[k], odd[k]) for k in range(4)] + [sub(even[k], odd[k]) for k in range(4)]


def finish_columns(rows, tables, wiener, out):
    lines = []
    for r in range(8):
        at = slice(r * 256, r * 256 + 256)
        both = jnp.concatenate(
            [jnp.transpose(rows[at, 0:128])[0:96], jnp.transpose(rows[at, 128:256])[0:96]], axis=0
        )
        upper = both.astype(BF16)
        stacked = jnp.concatenate([upper, (both - upper.astype(F32)).astype(BF16)], axis=0)
        waves = []
        for w in range(2):
            wide = dot(stacked, tables[0, r, w])
            waves.append(wide[0:192] + wide[192:384] + dot(upper, tables[1, r, w]))
        lines.append((waves[0][0:96] + waves[1][96:192], waves[0][96:192] - waves[1][0:96]))
    scale = 1.0 / math.sqrt(ROWS * COLS)
    for k, (real, imag) in enumerate(eighth(lines)):
        at = slice(k * 256, k * 256 + 256)
        for s in range(3):
            gain = wiener[s, :, at] * scale
            out[0, s, :, at] = real[s * 32 : s * 32 + 32] * gain
            out[1, s, :, at] = imag[s * 32 : s * 32 + 32] * gain


def map_kernel(
    timeline_in, pointing_in, plate_in, det_angle_in, det_weight_in, taps_in, owner_in, block_in,
    wiener_in, tables_in, out,
    rows, wiener, tables,
    plate, det_angle, det_weight, taps, owner, block, fetched,
    window, toep, trig, vals, pixels, spread, low_hot, local, gathered, meta, basis, turn,
    halo_send, halo_recv, m1_send, m1_recv, m2_send, m2_recv,
    p1_send, p1_recv, p2_send, p2_recv, sib_send, sib_recv,
):
    band = lax.axis_index("band")
    me = lax.axis_index("tm")
    y = me // 16
    z = (me // 2) % SIDE
    c = me % 2
    zc = me % 16

    def dev(yy, zz, cc):
        return (band, (yy % SIDE) * 16 + (zz % SIDE) * 2 + cc)

    def fetch(k, src, dst):
        copy = pltpu.make_async_copy(src, dst, fetched.at[k])
        copy.start()
        return copy

    own = window.at[pl.ds(TS, TS)]
    fetch_codes = [fetch(0, owner_in, owner), fetch(1, block_in, block)]
    fetch_samples = fetch(2, timeline_in, own)
    fetch_rest = [
        fetch(3, plate_in, plate),
        fetch(4, det_angle_in, det_angle),
        fetch(5, det_weight_in, det_weight),
        fetch(6, taps_in, taps),
    ]
    fetch_pixels = [
        fetch(7 + half, pointing_in.at[:, pl.ds(half * 128, 128)], pixels.at[half]) for half in range(2)
    ]

    right, left = (band, (me + 1) % N_TM), (band, (me + N_TM - 1) % N_TM)
    plane = [(band, y * 16 + (zc + k) % 16) for k in range(1, 16)]
    column = [dev(y + k, z, c) for k in range(1, SIDE)]
    barrier = pltpu.get_barrier_semaphore()
    for other in plane + column + [right, left]:
        pl.semaphore_signal(barrier, inc=1, device_id=other, device_id_type=MESH)

    for copy in fetch_codes:
        copy.wait()
    lane = iota((NTILE, 128), 1)
    q, a = (lane % NTILE) // 8, lane % 8
    wanted = ((q // 2) * 8 + a) * 2 + q % 2
    place = jnp.where((lane // NTILE == c) & (wanted == iota((NTILE, 128), 0)), 1.0, 0.0)
    sub = iota((8, NTILE), 0)
    parts = jnp.where(
        sub == 0, owner[...], jnp.where(sub == 1, block[...] // 32, block[...] % 32)
    ).astype(F32)
    spots = dot(parts.astype(BF16), place.astype(BF16)).astype(jnp.int32)
    meta[y, zc] = (spots[0:1] * 16 + spots[1:2]) * 32 + spots[2:3]

    fetch_samples.wait()
    pl.semaphore_wait(barrier, 24)

    def remote(src, dst, send, recv, to):
        copy = pltpu.make_async_remote_copy(
            src_ref=src, dst_ref=dst, send_sem=send, recv_sem=recv, device_id=to, device_id_type=MESH
        )
        copy.start()
        return copy

    pending = []
    halo = [
        remote(own, window.at[pl.ds(0, TS)], halo_send.at[0], halo_recv.at[0], right),
        remote(own, window.at[pl.ds(2 * TS, TS)], halo_send.at[1], halo_recv.at[1], left),
    ]
    first_meta = [
        remote(meta.at[y, zc], meta.at[y, zc], m1_send.at[k], m1_recv.at[k], to)
        for k, to in enumerate(plane)
    ]

    fetch_late = [fetch(9, wiener_in, wiener), fetch(10, tables_in, tables)]
    for copy in fetch_rest:
        copy.wait()
    band_rows = jnp.broadcast_to(taps[...], (256, TAPS_PAD))
    toep[...] = pltpu.roll(band_rows, 0, 1, stride=1, stride_axis=0).astype(BF16)
    plate_cos, plate_sin = jnp.cos(4.0 * plate[...]), jnp.sin(4.0 * plate[...])
    det_cos, det_sin = jnp.cos(2.0 * det_angle[...]), jnp.sin(2.0 * det_angle[...])
    for part in range(4):
        times = slice(part * 128, part * 128 + 128)
        cos_t = jnp.transpose(jnp.broadcast_to(plate_cos[part : part + 1], (128, 128)))
        sin_t = jnp.transpose(jnp.broadcast_to(plate_sin[part : part + 1], (128, 128)))
        for half in range(2):
            lanes = slice(half * 128, half * 128 + 128)
            trig[0, times, lanes] = cos_t * det_cos[:, lanes] - sin_t * det_sin[:, lanes]
            trig[1, times, lanes] = sin_t * det_cos[:, lanes] + cos_t * det_sin[:, lanes]

    rows[...] = jnp.zeros_like(rows)
    for copy in first_meta:
        copy.wait_recv()
    second_meta = [
        remote(meta.at[y], meta.at[y], m2_send.at[k], m2_recv.at[k], to)
        for k, to in enumerate(column)
    ]
    for copy in halo:
        copy.wait_recv()

    @pl.when(me == 0)
    def _():
        window[0:TS, :] = jnp.zeros((TS, DET), BF16)

    @pl.when(me == N_TM - 1)
    def _():
        window[2 * TS : 3 * TS, :] = jnp.zeros((TS, DET), BF16)

    for part in range(2):
        times = slice(part * 256, part * 256 + 256)
        filtered = dot(toep[...], window[part * 256 : part * 256 + TAPS_PAD, :])
        weighted = det_weight[...] * filtered
        for half in range(2):
            lanes = slice(half * 128, half * 128 + 128)
            vals[half, times, :] = weighted[:, lanes]
            vals[2 + half, times, :] = weighted[:, lanes] * trig[0, times, lanes]
            vals[4 + half, times, :] = weighted[:, lanes] * trig[1, times, lanes]

    for copy in fetch_pixels:
        copy.wait()
    lane = iota((8, 128), 1)
    pick = (lane // 8) * 8 + iota((8, 128), 0)

    def bin_tiles(q, carry):
        first = (q // 2) * 128
        for t in range(PIECE):
            where = pl.ds(first + t, 8, stride=PIECE)
            pixel = pixels[q % 2, where, :]
            high, low = pixel // 16, pixel % 16
            value = [vals[2 * s + q % 2, where, :] for s in range(3)]
            at = slice(t * 128, t * 128 + 128)
            for pair in range(12):
                both = []
                for k in (2 * pair, 2 * pair + 1):
                    both.append(jnp.where(high == k // 3, value[k % 3], 0.0))
                spread[pair * 16 : pair * 16 + 16, at] = jnp.concatenate(both, axis=0).astype(BF16)
            for pair in range(8):
                both = [jnp.where(low == k, 1.0, 0.0) for k in (2 * pair, 2 * pair + 1)]
                low_hot[pair * 16 : pair * 16 + 16, at] = jnp.concatenate(both, axis=0).astype(BF16)
        crossed = dot(spread[...], low_hot[...], ((1,), (1,)))
        for s in range(3):
            total = jnp.zeros((8, 128), F32)
            for h in range(8):
                k = h * 3 + s
                own = jnp.take_along_axis(crossed[k * 8 : k * 8 + 8], pick, axis=1)
                total = jnp.where(lane % 8 == h, own, total)
            local[pl.ds(pl.multiple_of(q * 8, 8), 8), s * 128 : s * 128 + 128] = total
        return carry

    lax.fori_loop(0, 8, bin_tiles, 0)

    for copy in second_meta:
        copy.wait_recv()
    pending += halo + first_meta + second_meta

    c1, c0 = c, 1 - c
    up = dev(y + c0, z + c1, c)
    down = dev(y + SIDE - c0, z + SIDE - c1, c)
    peers = [dev(y + c1 * k, z + c0 * k, c) for k in range(1, SIDE)]
    sibling = dev(y, z, 1 - c)

    def chip(d2, d1):
        return ((y + 16 - c1 * d1 - c0 * d2) % SIDE) * SIDE + (z + 16 - c0 * d1 - c1 * d2) % SIDE

    def sibling_chip(d2, d1):
        return ((y + 16 - c0 * d1 - c1 * d2) % SIDE) * SIDE + (z + 16 - c1 * d1 - c0 * d2) % SIDE

    half = pl.ds(pl.multiple_of(c * NTILE, NTILE), NTILE)
    gathered[y * SIDE + z, half] = local[...].astype(BF16)

    def carry(d2, d1, send, recv, to):
        piece = gathered.at[chip(d2, d1), half]
        return pltpu.make_async_remote_copy(
            src_ref=piece, dst_ref=piece, send_sem=send, recv_sem=recv, device_id=to, device_id_type=MESH
        )

    def to_peer(k):
        return carry(0, 0, p1_send.at[k], p1_recv.at[k], peers[k - 1])

    def to_line(d2, d1, step):
        to = up if step == 1 else down
        at = ((d2 + step) % SIDE) * SIDE + d1
        return carry(d2, d1, p2_send.at[at], p2_recv.at[at], to)

    def to_sibling(d2, d1):
        at = d2 * SIDE + d1
        return carry(d2, d1, sib_send.at[at], sib_recv.at[at], sibling)

    to_line(0, 0, 1).start()
    to_line(0, 0, 7).start()
    for k in (1, 2, 3, 7, 6, 5, 4):
        to_peer(k).start()
    to_sibling(0, 0).start()

    row = iota((BPIX, 128), 0)
    lane = iota((BPIX, 128), 1)
    pixel = (row % 8) * 16 + row // 8
    step = (((me * 32 + lane % 32) * pixel) % COLS).astype(F32) * (2.0 * math.pi / COLS)
    cos_x, sin_x = jnp.cos(step), jnp.sin(step)
    for s in range(3):
        mine = lane // 32 == s
        whole = jnp.concatenate([jnp.where(mine, cos_x, 0.0), jnp.where(mine, -sin_x, 0.0)], axis=1)
        high = whole.astype(BF16)
        basis[s * 128 : s * 128 + 128, :] = high
        basis[384 + s * 128 : 384 + s * 128 + 128, :] = (whole - high.astype(F32)).astype(BF16)
    step = ((iota((32, 128), 0) * (iota((32, 128), 1) % 32)) % 32).astype(F32) * (2.0 * math.pi / 32)
    whole = jnp.concatenate([jnp.cos(step), jnp.sin(step)], axis=1)
    high = whole.astype(BF16)
    turn[0:32, :] = high
    turn[32:64, :] = (whole - high.astype(F32)).astype(BF16)

    for d1 in (1, 2, 3, 7, 6, 5, 4):
        to_peer(d1).wait_recv()
        to_line(0, d1, 1).start()
        to_line(0, d1, 7).start()
        to_sibling(0, d1).start()

    def arrive(d2, d1, step):
        to_line((d2 + SIDE - step) % SIDE, d1, step).wait_recv()

    def members(g):
        k = (g + 1) // 2
        single = (7 - g % 7) // 7
        for e in range(8):
            sign, i = e // 4, e % 4
            d2 = (k + sign * (8 - 2 * k)) % SIDE
            d1 = (single * sign + (1 - single) * ((g + 1) % 2)) * 4 + i
            yield d2, d1

    key_rows = iota((256, 1024), 0).astype(F32).astype(BF16)
    turn_rows = iota((64, 1024), 0) % 32

    def each_group(g, state):
        k = 1 + g // 2

        @pl.when(g < 6)
        def _():
            for i in range(4):
                d1 = (g % 2) * 4 + i
                for step in (1, 7):
                    d2 = k if step == 1 else SIDE - k
                    arrive(d2, d1, step)

                    @pl.when(k < 3)
                    def _():
                        to_line(d2, d1, step).start()

                    @pl.when((k == 3) & (g % 2 == (0 if step == 1 else 1)))
                    def _():
                        to_line(d2, d1, step).start()

                    to_sibling(d2, d1).start()

        @pl.when(g == 6)
        def _():
            for d1 in (0, 4, 1, 5, 2, 6, 3, 7):
                arrive(4, d1, 1 if d1 < 4 else 7)
                to_sibling(4, d1).start()

        tiles, codes = [], []
        for d2, d1 in members(g):
            to_sibling(d2, d1).wait_recv()
            mine, other = chip(d2, d1), sibling_chip(d2, d1)
            first, second = mine * c0 + other * c1, mine * c1 + other * c0
            tiles += [gathered[first, 0:NTILE], gathered[second, NTILE : 2 * NTILE]]
            codes.append(
                meta[first // SIDE, (first % SIDE) * 2] + meta[second // SIDE, (second % SIDE) * 2 + 1]
            )
        tiles, codes = jnp.concatenate(tiles, axis=0), jnp.concatenate(codes, axis=1)
        spectra = dot(tiles, basis[0:384]) + dot(tiles, basis[384:768])
        turn_hot = jnp.where(turn_rows == codes % 32, 1.0, 0.0).astype(BF16)
        turned = dot(turn_hot, turn[...], ((0,), (0,)))
        real, imag = spectra[:, 0:128], spectra[:, 128:256]
        cos_b, sin_b = turned[:, 0:128], turned[:, 128:256]
        moved = jnp.concatenate(
            [real * cos_b + imag * sin_b, imag * cos_b - real * sin_b], axis=1
        ).astype(BF16)
        map_row = codes // 32
        low, high = map_row % 8, map_row // 8
        for r in range(8):
            key = jnp.where(low == r, high, -1).astype(F32).astype(BF16)
            hot = jnp.where(key_rows == key, jnp.bfloat16(1), jnp.bfloat16(0))
            rows[r * 256 : r * 256 + 256, :] += dot(hot, moved)
        return state

    lax.fori_loop(0, 8, each_group, 0)

    for copy in fetch_late:
        copy.wait()
    finish_columns(rows, tables, wiener, out)

    for copy in pending:
        copy.wait_send()
    for k in range(1, 8):
        to_peer(k).wait_send()

    def sent(n, state):
        d2, d1 = n // SIDE, n % SIDE
        to_sibling(d2, d1).wait_send()

        @pl.when(d2 > 0)
        def _():
            to_line((d2 + SIDE - 1) % SIDE, d1, 1).wait_send()

        return state

    lax.fori_loop(0, 64, sent, 0)


def column_tables():
    r0 = np.arange(256)[None, :, None]
    r1 = np.arange(8)[:, None, None]
    k = np.arange(256)[None, None, :]
    phase = (k * (r1 + 8 * r0) % ROWS) * (2.0 * np.pi / ROWS)
    table = np.stack([np.cos(phase), np.sin(phase)], axis=1)
    high = table.astype(BF16)
    low = (table - high.astype(np.float64)).astype(BF16)
    return np.stack([high, low])


def body(timeline, pointing, plate_angle, detector_angle, detector_weight, kernel, tile_owner, tile_block, wiener):
    taps = jnp.pad(kernel.astype(F32), (0, TAPS_PAD - kernel.shape[0])).reshape(1, TAPS_PAD)
    vmem = pl.BlockSpec(memory_space=pltpu.VMEM)
    dma = pltpu.SemaphoreType.DMA
    return pl.pallas_call(
        map_kernel,
        out_shape=jax.ShapeDtypeStruct((2, 3, 32, ROWS), F32),
        in_specs=[pl.BlockSpec(memory_space=pl.ANY)] * 10,
        out_specs=vmem,
        scratch_shapes=[
            pltpu.VMEM((ROWS, 256), F32),
            pltpu.VMEM((3, 32, ROWS), F32),
            pltpu.VMEM((2, 8, 2, 256, 256), BF16),
            pltpu.VMEM((4, 128), F32),
            pltpu.VMEM((1, DET), F32),
            pltpu.VMEM((1, DET), F32),
            pltpu.VMEM((1, TAPS_PAD), F32),
            pltpu.VMEM((1, NTILE), jnp.int32),
            pltpu.VMEM((1, NTILE), jnp.int32),
            dma((11,)),
            pltpu.VMEM((3 * TS, DET), BF16),
            pltpu.VMEM((256, TAPS_PAD), BF16),
            pltpu.VMEM((2, TS, DET), F32),
            pltpu.VMEM((6, TS, 128), F32),
            pltpu.VMEM((2, TS, 128), jnp.int32),
            pltpu.VMEM((192, PIECE * DGRP), BF16),
            pltpu.VMEM((128, PIECE * DGRP), BF16),
            pltpu.VMEM((NTILE, 384), F32),
            pltpu.VMEM((64, 2 * NTILE, 384), BF16),
            pltpu.VMEM((8, 16, 1, 128), jnp.int32),
            pltpu.VMEM((768, 256), BF16),
            pltpu.VMEM((64, 256), BF16),
            dma((2,)), dma((2,)), dma((15,)), dma((15,)), dma((7,)), dma((7,)),
            dma((8,)), dma((8,)), dma((64,)), dma((64,)), dma((64,)), dma((64,)),
        ],
        compiler_params=pltpu.CompilerParams(
            collective_id=0, has_side_effects=True, vmem_limit_bytes=64 << 20
        ),
        cost_estimate=pl.CostEstimate(flops=20 << 30, bytes_accessed=4 << 20, transcendentals=1 << 20),
    )(
        timeline,
        pointing,
        plate_angle.reshape(4, 128),
        detector_angle.reshape(1, DET),
        detector_weight.reshape(1, DET),
        taps,
        tile_owner.reshape(1, NTILE),
        tile_block.reshape(1, NTILE),
        wiener,
        jnp.asarray(column_tables()),
    )


def solution(mesh):
    placed = (
        P("tm", "band"),
        P("tm", "band"),
        P("tm"),
        P("band"),
        P("band"),
        P("band"),
        P("tm", "band"),
        P("tm", "band"),
        P("band", "tm", None),
    )
    return jax.shard_map(
        body, mesh=mesh, in_specs=placed, out_specs=P(None, "band", "tm", None), check_vma=False
    )
```

```python
import functools
import math

import jax
import jax.numpy as jnp
import numpy as np
from jax import lax
from jax.experimental import pallas as pl
from jax.experimental.pallas import tpu as pltpu
from jax.sharding import PartitionSpec as P

DET = 256
TS = 512
PIECE = 16
DGRP = 128
BPIX = 128
ROWS = 2048
COLS = 4096
NTILE = 64
N_TM = 128
SIDE = 8
TAPS_PAD = 1280
TAPS_ROW = 2048
MESH = pl.DeviceIdType.MESH
F32 = jnp.float32
BF16 = jnp.bfloat16


def dot(a, b, dims=((1,), (0,))):
    return lax.dot_general(a, b, (dims, ((), ())), preferred_element_type=F32)


def iota(shape, axis):
    return lax.broadcasted_iota(jnp.int32, shape, axis)


def eighth(parts):
    def add(u, v):
        return (u[0] + v[0], u[1] + v[1])

    def sub(u, v):
        return (u[0] - v[0], u[1] - v[1])

    def turn(u):
        return (u[1], -u[0])

    def four(u):
        s, d, t, e = add(u[0], u[2]), sub(u[0], u[2]), add(u[1], u[3]), turn(sub(u[1], u[3]))
        return [add(s, t), add(d, e), sub(s, t), sub(d, e)]

    even, odd = four(parts[0::2]), four(parts[1::2])
    h = math.sqrt(0.5)
    odd[1] = ((odd[1][0] + odd[1][1]) * h, (odd[1][1] - odd[1][0]) * h)
    odd[2] = turn(odd[2])
    odd[3] = ((odd[3][1] - odd[3][0]) * h, (-odd[3][0] - odd[3][1]) * h)
    return [add(even[k], odd[k]) for k in range(4)] + [sub(even[k], odd[k]) for k in range(4)]


def finish_columns(rows, tables, wiener, out):
    lines = []
    for r in range(8):
        at = slice(r * 256, r * 256 + 256)
        both = jnp.concatenate(
            [jnp.transpose(rows[at, 0:128])[0:96], jnp.transpose(rows[at, 128:256])[0:96]], axis=0
        )
        upper = both.astype(BF16)
        stacked = jnp.concatenate([upper, (both - upper.astype(F32)).astype(BF16)], axis=0)
        waves = []
        for w in range(2):
            wide = dot(stacked, tables[0, r, w])
            waves.append(wide[0:192] + wide[192:384] + dot(upper, tables[1, r, w]))
        lines.append((waves[0][0:96] + waves[1][96:192], waves[0][96:192] - waves[1][0:96]))
    scale = 1.0 / math.sqrt(ROWS * COLS)
    for k, (real, imag) in enumerate(eighth(lines)):
        at = slice(k * 256, k * 256 + 256)
        for s in range(3):
            gain = wiener[s, :, at] * scale
            out[0, s, :, at] = real[s * 32 : s * 32 + 32] * gain
            out[1, s, :, at] = imag[s * 32 : s * 32 + 32] * gain


def map_kernel(
    timeline_in, pointing_in, plate_in, det_angle_in, det_weight_in, taps_in, owner_in, block_in,
    wiener_in, tables_in, out,
    rows, wiener, tables,
    plate, det_angle, det_weight, taps, owner, block, fetched,
    window, toep, trig, vals, pixels, spread, low_hot, local, gathered, meta, basis, turn,
    halo_send, halo_recv, m1_send, m1_recv, m2_send, m2_recv,
    p1_send, p1_recv, p2_send, p2_recv, sib_send, sib_recv,
):
    band = lax.axis_index("band")
    me = lax.axis_index("tm")
    y = me // 16
    z = (me // 2) % SIDE
    c = me % 2
    zc = me % 16

    def dev(yy, zz, cc):
        return (band, (yy % SIDE) * 16 + (zz % SIDE) * 2 + cc)

    def fetch(k, src, dst):
        copy = pltpu.make_async_copy(src, dst, fetched.at[k])
        copy.start()
        return copy

    own = window.at[pl.ds(TS, TS)]
    fetch_codes = [fetch(0, owner_in, owner), fetch(1, block_in, block)]
    fetch_samples = fetch(2, timeline_in, own)
    fetch_rest = [
        fetch(3, plate_in, plate),
        fetch(4, det_angle_in, det_angle),
        fetch(5, det_weight_in, det_weight),
        fetch(6, taps_in, taps),
    ]
    fetch_pixels = [
        fetch(7 + half, pointing_in.at[:, pl.ds(half * 128, 128)], pixels.at[half]) for half in range(2)
    ]

    right, left = (band, (me + 1) % N_TM), (band, (me + N_TM - 1) % N_TM)
    plane = [(band, y * 16 + (zc + k) % 16) for k in range(1, 16)]
    column = [dev(y + k, z, c) for k in range(1, SIDE)]
    barrier = pltpu.get_barrier_semaphore()
    for other in plane + column + [right, left]:
        pl.semaphore_signal(barrier, inc=1, device_id=other, device_id_type=MESH)

    for copy in fetch_codes:
        copy.wait()
    lane = iota((NTILE, 128), 1)
    q, a = (lane % NTILE) // 8, lane % 8
    wanted = ((q // 2) * 8 + a) * 2 + q % 2
    place = jnp.where((lane // NTILE == c) & (wanted == iota((NTILE, 128), 0)), 1.0, 0.0)
    sub = iota((8, NTILE), 0)
    parts = jnp.where(
        sub == 0, owner[...], jnp.where(sub == 1, block[...] // 32, block[...] % 32)
    ).astype(F32)
    spots = dot(parts.astype(BF16), place.astype(BF16)).astype(jnp.int32)
    meta[y, zc] = (spots[0:1] * 16 + spots[1:2]) * 32 + spots[2:3]

    fetch_samples.wait()
    pl.semaphore_wait(barrier, 24)

    def remote(src, dst, send, recv, to):
        copy = pltpu.make_async_remote_copy(
            src_ref=src, dst_ref=dst, send_sem=send, recv_sem=recv, device_id=to, device_id_type=MESH
        )
        copy.start()
        return copy

    pending = []
    halo = [
        remote(own, window.at[pl.ds(0, TS)], halo_send.at[0], halo_recv.at[0], right),
        remote(own, window.at[pl.ds(2 * TS, TS)], halo_send.at[1], halo_recv.at[1], left),
    ]
    first_meta = [
        remote(meta.at[y, zc], meta.at[y, zc], m1_send.at[k], m1_recv.at[k], to)
        for k, to in enumerate(plane)
    ]

    fetch_late = [fetch(9, wiener_in, wiener), fetch(10, tables_in, tables)]
    for copy in fetch_rest:
        copy.wait()
    band_rows = jnp.broadcast_to(taps[:, 0:TAPS_PAD], (256, TAPS_PAD))
    toep[...] = pltpu.roll(band_rows, 0, 1, stride=1, stride_axis=0).astype(BF16)
    plate_cos, plate_sin = jnp.cos(4.0 * plate[...]), jnp.sin(4.0 * plate[...])
    det_cos, det_sin = jnp.cos(2.0 * det_angle[...]), jnp.sin(2.0 * det_angle[...])
    for part in range(4):
        times = slice(part * 128, part * 128 + 128)
        cos_t = jnp.transpose(jnp.broadcast_to(plate_cos[part : part + 1], (128, 128)))
        sin_t = jnp.transpose(jnp.broadcast_to(plate_sin[part : part + 1], (128, 128)))
        for half in range(2):
            lanes = slice(half * 128, half * 128 + 128)
            trig[0, times, lanes] = cos_t * det_cos[:, lanes] - sin_t * det_sin[:, lanes]
            trig[1, times, lanes] = sin_t * det_cos[:, lanes] + cos_t * det_sin[:, lanes]

    rows[...] = jnp.zeros_like(rows)
    for copy in halo:
        copy.wait_recv()

    @pl.when(me == 0)
    def _():
        window[0:TS, :] = jnp.zeros((TS, DET), BF16)

    @pl.when(me == N_TM - 1)
    def _():
        window[2 * TS : 3 * TS, :] = jnp.zeros((TS, DET), BF16)

    for part in range(2):
        times = slice(part * 256, part * 256 + 256)
        filtered = dot(toep[...], window[part * 256 : part * 256 + TAPS_PAD, :])
        weighted = det_weight[...] * filtered
        for half in range(2):
            lanes = slice(half * 128, half * 128 + 128)
            vals[half, times, :] = weighted[:, lanes]
            vals[2 + half, times, :] = weighted[:, lanes] * trig[0, times, lanes]
            vals[4 + half, times, :] = weighted[:, lanes] * trig[1, times, lanes]

    for copy in fetch_pixels:
        copy.wait()
    lane = iota((8, 128), 1)
    pick = (lane // 8) * 8 + iota((8, 128), 0)

    def bin_tiles(q, carry):
        first = (q // 2) * 128
        for t in range(PIECE):
            where = pl.ds(first + t, 8, stride=PIECE)
            pixel = pixels[q % 2, where, :]
            high, low = pixel // 16, pixel % 16
            value = [vals[2 * s + q % 2, where, :] for s in range(3)]
            at = slice(t * 128, t * 128 + 128)
            for pair in range(12):
                both = []
                for k in (2 * pair, 2 * pair + 1):
                    both.append(jnp.where(high == k // 3, value[k % 3], 0.0))
                spread[pair * 16 : pair * 16 + 16, at] = jnp.concatenate(both, axis=0).astype(BF16)
            for pair in range(8):
                both = [jnp.where(low == k, 1.0, 0.0) for k in (2 * pair, 2 * pair + 1)]
                low_hot[pair * 16 : pair * 16 + 16, at] = jnp.concatenate(both, axis=0).astype(BF16)
        crossed = dot(spread[...], low_hot[...], ((1,), (1,)))
        for s in range(3):
            total = jnp.zeros((8, 128), F32)
            for h in range(8):
                k = h * 3 + s
                own = jnp.take_along_axis(crossed[k * 8 : k * 8 + 8], pick, axis=1)
                total = jnp.where(lane % 8 == h, own, total)
            local[pl.ds(pl.multiple_of(q * 8, 8), 8), s * 128 : s * 128 + 128] = total
        return carry

    lax.fori_loop(0, 8, bin_tiles, 0)

    pending += halo + first_meta

    c1, c0 = c, 1 - c
    up = dev(y + c0, z + c1, c)
    down = dev(y + SIDE - c0, z + SIDE - c1, c)
    peers = [dev(y + c1 * k, z + c0 * k, c) for k in range(1, SIDE)]
    sibling = dev(y, z, 1 - c)

    gathered[c, 0, 0] = local[...].astype(BF16)

    def carry(src, dst, send, recv, to):
        return pltpu.make_async_remote_copy(
            src_ref=src, dst_ref=dst, send_sem=send, recv_sem=recv, device_id=to, device_id_type=MESH
        )

    def four(d2, h):
        return gathered.at[c, d2, pl.ds(pl.multiple_of(h * 4, 4), 4)]

    def to_peer(k):
        src, dst = gathered.at[c, 0, 0], gathered.at[c, 0, k]
        return carry(src, dst, p1_send.at[k], p1_recv.at[k], peers[k - 1])

    def to_line(d2, h, step):
        to, then = up if step == 1 else down, (d2 + step) % SIDE
        at = then * 2 + h
        return carry(four(d2, h), four(then, h), p2_send.at[at], p2_recv.at[at], to)

    def to_sibling(d2, h):
        at = d2 * 2 + h
        return carry(four(d2, h), four(d2, h), sib_send.at[at], sib_recv.at[at], sibling)

    for k in (1, 2, 3, 7, 6, 5, 4):
        to_peer(k).start()
    for copy in first_meta:
        copy.wait_recv()
    second_meta = [
        remote(meta.at[y], meta.at[y], m2_send.at[k], m2_recv.at[k], to)
        for k, to in enumerate(column)
    ]
    pending += second_meta

    row = iota((BPIX, 128), 0)
    lane = iota((BPIX, 128), 1)
    pixel = (row % 8) * 16 + row // 8
    step = (((me * 32 + lane % 32) * pixel) % COLS).astype(F32) * (2.0 * math.pi / COLS)
    cos_x, sin_x = jnp.cos(step), jnp.sin(step)
    for s in range(3):
        mine = lane // 32 == s
        whole = jnp.concatenate([jnp.where(mine, cos_x, 0.0), jnp.where(mine, -sin_x, 0.0)], axis=1)
        high = whole.astype(BF16)
        basis[s * 128 : s * 128 + 128, :] = high
        basis[384 + s * 128 : 384 + s * 128 + 128, :] = (whole - high.astype(F32)).astype(BF16)
    step = ((iota((32, 128), 0) * (iota((32, 128), 1) % 32)) % 32).astype(F32) * (2.0 * math.pi / 32)
    whole = jnp.concatenate([jnp.cos(step), jnp.sin(step)], axis=1)
    high = whole.astype(BF16)
    turn[0:32, :] = high
    turn[32:64, :] = (whole - high.astype(F32)).astype(BF16)

    for h in range(2):
        for d1 in ((1, 2, 3), (7, 6, 5, 4))[h]:
            to_peer(d1).wait_recv()
        to_line(0, h, 1).start()
        to_line(0, h, 7).start()
        to_sibling(0, h).start()
    for copy in second_meta:
        copy.wait_recv()

    def arrive(d2, h, step):
        to_line((d2 + SIDE - step) % SIDE, h, step).wait_recv()

    def members(g):
        k = (g + 1) // 2
        single = (7 - g % 7) // 7
        for sign in range(2):
            yield (k + sign * (8 - 2 * k)) % SIDE, single * sign + (1 - single) * ((g + 1) % 2)

    key_rows = iota((256, 1024), 0).astype(F32).astype(BF16)
    turn_rows = iota((64, 1024), 0) % 32

    def each_group(g, state):
        k, h = 1 + g // 2, g % 2

        @pl.when(g < 6)
        def _():
            for step in (1, 7):
                d2 = k if step == 1 else SIDE - k
                arrive(d2, h, step)

                @pl.when(k < 3)
                def _():
                    to_line(d2, h, step).start()

                @pl.when((k == 3) & (h == (0 if step == 1 else 1)))
                def _():
                    to_line(d2, h, step).start()

                to_sibling(d2, h).start()

        @pl.when(g == 6)
        def _():
            for last in range(2):
                arrive(4, last, 1 if last == 0 else 7)
                to_sibling(4, last).start()

        tiles, codes = [], []
        for d2, quad in members(g):
            to_sibling(d2, quad).wait_recv()
            for i in range(4):
                d1 = quad * 4 + i
                tiles += [gathered[0, d2, d1], gathered[1, d2, d1]]
                far, near = (y + SIDE - d2) % SIDE, (z + SIDE - d1) % SIDE
                across, along = (y + SIDE - d1) % SIDE, (z + SIDE - d2) % SIDE
                codes.append(meta[far, near * 2] + meta[across, along * 2 + 1])
        tiles, codes = jnp.concatenate(tiles, axis=0), jnp.concatenate(codes, axis=1)
        spectra = dot(tiles, basis[0:384]) + dot(tiles, basis[384:768])
        turn_hot = jnp.where(turn_rows == codes % 32, 1.0, 0.0).astype(BF16)
        turned = dot(turn_hot, turn[...], ((0,), (0,)))
        real, imag = spectra[:, 0:128], spectra[:, 128:256]
        cos_b, sin_b = turned[:, 0:128], turned[:, 128:256]
        moved = jnp.concatenate(
            [real * cos_b + imag * sin_b, imag * cos_b - real * sin_b], axis=1
        ).astype(BF16)
        map_row = codes // 32
        low, high = map_row % 8, map_row // 8
        for r in range(8):
            key = jnp.where(low == r, high, -1).astype(F32).astype(BF16)
            hot = jnp.where(key_rows == key, jnp.bfloat16(1), jnp.bfloat16(0))
            rows[r * 256 : r * 256 + 256, :] += dot(hot, moved)
        return state

    lax.fori_loop(0, 8, each_group, 0)

    for copy in fetch_late:
        copy.wait()
    finish_columns(rows, tables, wiener, out)

    for copy in pending:
        copy.wait_send()
    for k in range(1, 8):
        to_peer(k).wait_send()

    def sent(n, state):
        d2, h = n // 2, n % 2
        to_sibling(d2, h).wait_send()

        @pl.when(d2 > 0)
        def _():
            to_line((d2 + SIDE - 1) % SIDE, h, 1).wait_send()

        return state

    lax.fori_loop(0, 16, sent, 0)


def column_tables():
    r0 = np.arange(256)[None, :, None]
    r1 = np.arange(8)[:, None, None]
    k = np.arange(256)[None, None, :]
    phase = (k * (r1 + 8 * r0) % ROWS) * (2.0 * np.pi / ROWS)
    table = np.stack([np.cos(phase), np.sin(phase)], axis=1)
    high = table.astype(BF16)
    low = (table - high.astype(np.float64)).astype(BF16)
    return np.stack([high, low])


def body(timeline, pointing, plate_angle, detector_angle, detector_weight, kernel, tile_owner, tile_block, wiener):
    taps = jnp.pad(kernel.astype(F32), (0, TAPS_ROW - kernel.shape[0])).reshape(1, TAPS_ROW)
    vmem = pl.BlockSpec(memory_space=pltpu.VMEM)
    dma = pltpu.SemaphoreType.DMA
    return pl.pallas_call(
        map_kernel,
        out_shape=jax.ShapeDtypeStruct((2, 3, 32, ROWS), F32),
        in_specs=[pl.BlockSpec(memory_space=pl.ANY)] * 10,
        out_specs=vmem,
        scratch_shapes=[
            pltpu.VMEM((ROWS, 256), F32),
            pltpu.VMEM((3, 32, ROWS), F32),
            pltpu.VMEM((2, 8, 2, 256, 256), BF16),
            pltpu.VMEM((4, 128), F32),
            pltpu.VMEM((1, DET), F32),
            pltpu.VMEM((1, DET), F32),
            pltpu.VMEM((1, TAPS_ROW), F32),
            pltpu.VMEM((1, NTILE), jnp.int32),
            pltpu.VMEM((1, NTILE), jnp.int32),
            dma((11,)),
            pltpu.VMEM((3 * TS, DET), BF16),
            pltpu.VMEM((256, TAPS_PAD), BF16),
            pltpu.VMEM((2, TS, DET), F32),
            pltpu.VMEM((6, TS, 128), F32),
            pltpu.VMEM((2, TS, 128), jnp.int32),
            pltpu.VMEM((192, PIECE * DGRP), BF16),
            pltpu.VMEM((128, PIECE * DGRP), BF16),
            pltpu.VMEM((NTILE, 384), F32),
            pltpu.VMEM((2, SIDE, SIDE, NTILE, 384), BF16),
            pltpu.VMEM((8, 16, 1, 128), jnp.int32),
            pltpu.VMEM((768, 256), BF16),
            pltpu.VMEM((64, 256), BF16),
            dma((2,)), dma((2,)), dma((15,)), dma((15,)), dma((7,)), dma((7,)),
            dma((8,)), dma((8,)), dma((16,)), dma((16,)), dma((16,)), dma((16,)),
        ],
        compiler_params=pltpu.CompilerParams(
            collective_id=0, has_side_effects=True, vmem_limit_bytes=64 << 20
        ),
        cost_estimate=pl.CostEstimate(flops=20 << 30, bytes_accessed=4 << 20, transcendentals=1 << 20),
    )(
        timeline,
        pointing,
        plate_angle.reshape(4, 128),
        detector_angle.reshape(1, DET),
        detector_weight.reshape(1, DET),
        taps,
        tile_owner.reshape(1, NTILE),
        tile_block.reshape(1, NTILE),
        wiener,
        jnp.asarray(column_tables()),
    )


def solution(mesh):
    placed = (
        P("tm", "band"),
        P("tm", "band"),
        P("tm"),
        P("band"),
        P("band"),
        P("band"),
        P("tm", "band"),
        P("tm", "band"),
        P("band", "tm", None),
    )
    return jax.shard_map(
        body, mesh=mesh, in_specs=placed, out_specs=P(None, "band", "tm", None), check_vma=False
    )
```

```python
import functools
import math

import jax
import jax.numpy as jnp
import numpy as np
from jax import lax
from jax.experimental import pallas as pl
from jax.experimental.pallas import tpu as pltpu
from jax.sharding import PartitionSpec as P

DET = 256
TS = 512
PIECE = 16
DGRP = 128
BPIX = 128
ROWS = 2048
COLS = 4096
NTILE = 64
N_TM = 128
SIDE = 8
TAPS_PAD = 1280
TAPS_ROW = 2048
MESH = pl.DeviceIdType.MESH
F32 = jnp.float32
BF16 = jnp.bfloat16


def dot(a, b, dims=((1,), (0,))):
    return lax.dot_general(a, b, (dims, ((), ())), preferred_element_type=F32)


def iota(shape, axis):
    return lax.broadcasted_iota(jnp.int32, shape, axis)


def eighth(parts):
    def add(u, v):
        return (u[0] + v[0], u[1] + v[1])

    def sub(u, v):
        return (u[0] - v[0], u[1] - v[1])

    def turn(u):
        return (u[1], -u[0])

    def four(u):
        s, d, t, e = add(u[0], u[2]), sub(u[0], u[2]), add(u[1], u[3]), turn(sub(u[1], u[3]))
        return [add(s, t), add(d, e), sub(s, t), sub(d, e)]

    even, odd = four(parts[0::2]), four(parts[1::2])
    h = math.sqrt(0.5)
    odd[1] = ((odd[1][0] + odd[1][1]) * h, (odd[1][1] - odd[1][0]) * h)
    odd[2] = turn(odd[2])
    odd[3] = ((odd[3][1] - odd[3][0]) * h, (-odd[3][0] - odd[3][1]) * h)
    return [add(even[k], odd[k]) for k in range(4)] + [sub(even[k], odd[k]) for k in range(4)]


def finish_columns(rows, tables, out):
    lines = []
    for r in range(8):
        at = slice(r * 256, r * 256 + 256)
        both = jnp.concatenate(
            [jnp.transpose(rows[at, 0:128])[0:96], jnp.transpose(rows[at, 128:256])[0:96]], axis=0
        )
        upper = both.astype(BF16)
        stacked = jnp.concatenate([upper, (both - upper.astype(F32)).astype(BF16)], axis=0)
        waves = []
        for w in range(2):
            wide = dot(stacked, tables[0, r, w])
            waves.append(wide[0:192] + wide[192:384] + dot(upper, tables[1, r, w]))
        lines.append((waves[0][0:96] + waves[1][96:192], waves[0][96:192] - waves[1][0:96]))
    scale = 1.0 / math.sqrt(ROWS * COLS)
    for k, (real, imag) in enumerate(eighth(lines)):
        at = slice(k * 256, k * 256 + 256)
        for s in range(3):
            out[0, s, :, at] = real[s * 32 : s * 32 + 32] * scale
            out[1, s, :, at] = imag[s * 32 : s * 32 + 32] * scale


def map_kernel(
    timeline_in, pointing_in, plate_in, det_angle_in, det_weight_in, taps_in, owner_in, block_in,
    tables_in, out,
    rows, tables,
    plate, det_angle, det_weight, taps, owner, block, fetched,
    window, toep, trig, vals, pixels, spread, low_hot, local, gathered, meta, basis, turn,
    halo_send, halo_recv, m1_send, m1_recv, m2_send, m2_recv,
    p1_send, p1_recv, p2_send, p2_recv, sib_send, sib_recv,
):
    band = lax.axis_index("band")
    me = lax.axis_index("tm")
    y = me // 16
    z = (me // 2) % SIDE
    c = me % 2
    zc = me % 16

    def dev(yy, zz, cc):
        return (band, (yy % SIDE) * 16 + (zz % SIDE) * 2 + cc)

    def fetch(k, src, dst):
        copy = pltpu.make_async_copy(src, dst, fetched.at[k])
        copy.start()
        return copy

    own = window.at[pl.ds(TS, TS)]
    fetch_codes = [fetch(0, owner_in, owner), fetch(1, block_in, block)]
    fetch_samples = fetch(2, timeline_in, own)
    fetch_rest = [
        fetch(3, plate_in, plate),
        fetch(4, det_angle_in, det_angle),
        fetch(5, det_weight_in, det_weight),
        fetch(6, taps_in, taps),
    ]
    fetch_pixels = [
        fetch(7 + half, pointing_in.at[:, pl.ds(half * 128, 128)], pixels.at[half]) for half in range(2)
    ]

    right, left = (band, (me + 1) % N_TM), (band, (me + N_TM - 1) % N_TM)
    plane = [(band, y * 16 + (zc + k) % 16) for k in range(1, 16)]
    column = [dev(y + k, z, c) for k in range(1, SIDE)]
    barrier = pltpu.get_barrier_semaphore()
    for other in plane + column + [right, left]:
        pl.semaphore_signal(barrier, inc=1, device_id=other, device_id_type=MESH)

    for copy in fetch_codes:
        copy.wait()
    lane = iota((NTILE, 128), 1)
    q, a = (lane % NTILE) // 8, lane % 8
    wanted = ((q // 2) * 8 + a) * 2 + q % 2
    place = jnp.where((lane // NTILE == c) & (wanted == iota((NTILE, 128), 0)), 1.0, 0.0)
    sub = iota((8, NTILE), 0)
    parts = jnp.where(
        sub == 0, owner[...], jnp.where(sub == 1, block[...] // 32, block[...] % 32)
    ).astype(F32)
    spots = dot(parts.astype(BF16), place.astype(BF16)).astype(jnp.int32)
    meta[y, zc] = (spots[0:1] * 16 + spots[1:2]) * 32 + spots[2:3]

    fetch_samples.wait()
    pl.semaphore_wait(barrier, 24)

    def remote(src, dst, send, recv, to):
        copy = pltpu.make_async_remote_copy(
            src_ref=src, dst_ref=dst, send_sem=send, recv_sem=recv, device_id=to, device_id_type=MESH
        )
        copy.start()
        return copy

    pending = []
    halo = [
        remote(own, window.at[pl.ds(0, TS)], halo_send.at[0], halo_recv.at[0], right),
        remote(own, window.at[pl.ds(2 * TS, TS)], halo_send.at[1], halo_recv.at[1], left),
    ]
    first_meta = [
        remote(meta.at[y, zc], meta.at[y, zc], m1_send.at[k], m1_recv.at[k], to)
        for k, to in enumerate(plane)
    ]

    fetch_late = [fetch(9, tables_in, tables)]
    for copy in fetch_rest:
        copy.wait()
    band_rows = jnp.broadcast_to(taps[:, 0:TAPS_PAD], (256, TAPS_PAD))
    toep[...] = pltpu.roll(band_rows, 0, 1, stride=1, stride_axis=0).astype(BF16)
    plate_cos, plate_sin = jnp.cos(4.0 * plate[...]), jnp.sin(4.0 * plate[...])
    det_cos, det_sin = jnp.cos(2.0 * det_angle[...]), jnp.sin(2.0 * det_angle[...])
    for part in range(4):
        times = slice(part * 128, part * 128 + 128)
        cos_t = jnp.transpose(jnp.broadcast_to(plate_cos[part : part + 1], (128, 128)))
        sin_t = jnp.transpose(jnp.broadcast_to(plate_sin[part : part + 1], (128, 128)))
        for half in range(2):
            lanes = slice(half * 128, half * 128 + 128)
            trig[0, times, lanes] = cos_t * det_cos[:, lanes] - sin_t * det_sin[:, lanes]
            trig[1, times, lanes] = sin_t * det_cos[:, lanes] + cos_t * det_sin[:, lanes]

    rows[...] = jnp.zeros_like(rows)
    for copy in halo:
        copy.wait_recv()

    @pl.when(me == 0)
    def _():
        window[0:TS, :] = jnp.zeros((TS, DET), BF16)

    @pl.when(me == N_TM - 1)
    def _():
        window[2 * TS : 3 * TS, :] = jnp.zeros((TS, DET), BF16)

    for part in range(2):
        times = slice(part * 256, part * 256 + 256)
        filtered = dot(toep[...], window[part * 256 : part * 256 + TAPS_PAD, :])
        weighted = det_weight[...] * filtered
        for half in range(2):
            lanes = slice(half * 128, half * 128 + 128)
            vals[half, times, :] = weighted[:, lanes]
            vals[2 + half, times, :] = weighted[:, lanes] * trig[0, times, lanes]
            vals[4 + half, times, :] = weighted[:, lanes] * trig[1, times, lanes]

    for copy in fetch_pixels:
        copy.wait()
    lane = iota((8, 128), 1)
    pick = (lane // 8) * 8 + iota((8, 128), 0)

    def bin_tiles(q, carry):
        first = (q // 2) * 128
        for t in range(PIECE):
            where = pl.ds(first + t, 8, stride=PIECE)
            pixel = pixels[q % 2, where, :]
            high, low = pixel // 16, pixel % 16
            value = [vals[2 * s + q % 2, where, :] for s in range(3)]
            at = slice(t * 128, t * 128 + 128)
            for pair in range(12):
                both = []
                for k in (2 * pair, 2 * pair + 1):
                    both.append(jnp.where(high == k // 3, value[k % 3], 0.0))
                spread[pair * 16 : pair * 16 + 16, at] = jnp.concatenate(both, axis=0).astype(BF16)
            for pair in range(8):
                both = [jnp.where(low == k, 1.0, 0.0) for k in (2 * pair, 2 * pair + 1)]
                low_hot[pair * 16 : pair * 16 + 16, at] = jnp.concatenate(both, axis=0).astype(BF16)
        crossed = dot(spread[...], low_hot[...], ((1,), (1,)))
        for s in range(3):
            total = jnp.zeros((8, 128), F32)
            for h in range(8):
                k = h * 3 + s
                own = jnp.take_along_axis(crossed[k * 8 : k * 8 + 8], pick, axis=1)
                total = jnp.where(lane % 8 == h, own, total)
            local[pl.ds(pl.multiple_of(q * 8, 8), 8), s * 128 : s * 128 + 128] = total
        return carry

    lax.fori_loop(0, 8, bin_tiles, 0)

    pending += halo + first_meta

    c1, c0 = c, 1 - c
    up = dev(y + c0, z + c1, c)
    down = dev(y + SIDE - c0, z + SIDE - c1, c)
    peers = [dev(y + c1 * k, z + c0 * k, c) for k in range(1, SIDE)]
    sibling = dev(y, z, 1 - c)

    gathered[c, 0, 0] = local[...].astype(BF16)

    def carry(src, dst, send, recv, to):
        return pltpu.make_async_remote_copy(
            src_ref=src, dst_ref=dst, send_sem=send, recv_sem=recv, device_id=to, device_id_type=MESH
        )

    def four(d2, h):
        return gathered.at[c, d2, pl.ds(pl.multiple_of(h * 4, 4), 4)]

    def to_peer(k):
        src, dst = gathered.at[c, 0, 0], gathered.at[c, 0, k]
        return carry(src, dst, p1_send.at[k], p1_recv.at[k], peers[k - 1])

    def to_line(d2, h, step):
        to, then = up if step == 1 else down, (d2 + step) % SIDE
        at = then * 2 + h
        return carry(four(d2, h), four(then, h), p2_send.at[at], p2_recv.at[at], to)

    def to_sibling(d2, h):
        at = d2 * 2 + h
        return carry(four(d2, h), four(d2, h), sib_send.at[at], sib_recv.at[at], sibling)

    for k in (1, 2, 3, 7, 6, 5, 4):
        to_peer(k).start()
    for copy in first_meta:
        copy.wait_recv()
    second_meta = [
        remote(meta.at[y], meta.at[y], m2_send.at[k], m2_recv.at[k], to)
        for k, to in enumerate(column)
    ]
    pending += second_meta

    row = iota((BPIX, 128), 0)
    lane = iota((BPIX, 128), 1)
    pixel = (row % 8) * 16 + row // 8
    step = (((me * 32 + lane % 32) * pixel) % COLS).astype(F32) * (2.0 * math.pi / COLS)
    cos_x, sin_x = jnp.cos(step), jnp.sin(step)
    for s in range(3):
        mine = lane // 32 == s
        whole = jnp.concatenate([jnp.where(mine, cos_x, 0.0), jnp.where(mine, -sin_x, 0.0)], axis=1)
        high = whole.astype(BF16)
        basis[s * 128 : s * 128 + 128, :] = high
        basis[384 + s * 128 : 384 + s * 128 + 128, :] = (whole - high.astype(F32)).astype(BF16)
    step = ((iota((32, 128), 0) * (iota((32, 128), 1) % 32)) % 32).astype(F32) * (2.0 * math.pi / 32)
    whole = jnp.concatenate([jnp.cos(step), jnp.sin(step)], axis=1)
    high = whole.astype(BF16)
    turn[0:32, :] = high
    turn[32:64, :] = (whole - high.astype(F32)).astype(BF16)

    for h in range(2):
        for d1 in ((1, 2, 3), (7, 6, 5, 4))[h]:
            to_peer(d1).wait_recv()
        to_line(0, h, 1).start()
        to_line(0, h, 7).start()
        to_sibling(0, h).start()
    for copy in second_meta:
        copy.wait_recv()

    def arrive(d2, h, step):
        to_line((d2 + SIDE - step) % SIDE, h, step).wait_recv()

    def members(g):
        k = (g + 1) // 2
        single = (7 - g % 7) // 7
        for sign in range(2):
            yield (k + sign * (8 - 2 * k)) % SIDE, single * sign + (1 - single) * ((g + 1) % 2)

    key_rows = iota((256, 1024), 0).astype(F32).astype(BF16)
    turn_rows = iota((64, 1024), 0) % 32

    def each_group(g, state):
        k, h = 1 + g // 2, g % 2

        @pl.when(g < 6)
        def _():
            for step in (1, 7):
                d2 = k if step == 1 else SIDE - k
                arrive(d2, h, step)

                @pl.when(k < 3)
                def _():
                    to_line(d2, h, step).start()

                @pl.when((k == 3) & (h == (0 if step == 1 else 1)))
                def _():
                    to_line(d2, h, step).start()

                to_sibling(d2, h).start()

        @pl.when(g == 6)
        def _():
            for last in range(2):
                arrive(4, last, 1 if last == 0 else 7)
                to_sibling(4, last).start()

        tiles, codes = [], []
        for d2, quad in members(g):
            to_sibling(d2, quad).wait_recv()
            for i in range(4):
                d1 = quad * 4 + i
                tiles += [gathered[0, d2, d1], gathered[1, d2, d1]]
                far, near = (y + SIDE - d2) % SIDE, (z + SIDE - d1) % SIDE
                across, along = (y + SIDE - d1) % SIDE, (z + SIDE - d2) % SIDE
                codes.append(meta[far, near * 2] + meta[across, along * 2 + 1])
        tiles, codes = jnp.concatenate(tiles, axis=0), jnp.concatenate(codes, axis=1)
        spectra = dot(jnp.concatenate([tiles, tiles], axis=1), basis[...])
        turn_hot = jnp.where(turn_rows == codes % 32, 1.0, 0.0).astype(BF16)
        turned = dot(turn_hot, turn[...], ((0,), (0,)))
        real, imag = spectra[:, 0:128], spectra[:, 128:256]
        cos_b, sin_b = turned[:, 0:128], turned[:, 128:256]
        moved = jnp.concatenate(
            [real * cos_b + imag * sin_b, imag * cos_b - real * sin_b], axis=1
        ).astype(BF16)
        map_row = codes // 32
        low, high = map_row % 8, map_row // 8
        for r in range(8):
            key = jnp.where(low == r, high, -1).astype(F32).astype(BF16)
            hot = jnp.where(key_rows == key, jnp.bfloat16(1), jnp.bfloat16(0))
            rows[r * 256 : r * 256 + 256, :] += dot(hot, moved)
        return state

    lax.fori_loop(0, 8, each_group, 0)

    for copy in fetch_late:
        copy.wait()
    finish_columns(rows, tables, out)

    for copy in pending:
        copy.wait_send()
    for k in range(1, 8):
        to_peer(k).wait_send()

    def sent(n, state):
        d2, h = n // 2, n % 2
        to_sibling(d2, h).wait_send()

        @pl.when(d2 > 0)
        def _():
            to_line((d2 + SIDE - 1) % SIDE, h, 1).wait_send()

        return state

    lax.fori_loop(0, 16, sent, 0)


def column_tables():
    r0 = np.arange(256)[None, :, None]
    r1 = np.arange(8)[:, None, None]
    k = np.arange(256)[None, None, :]
    phase = (k * (r1 + 8 * r0) % ROWS) * (2.0 * np.pi / ROWS)
    table = np.stack([np.cos(phase), np.sin(phase)], axis=1)
    high = table.astype(BF16)
    low = (table - high.astype(np.float64)).astype(BF16)
    return np.stack([high, low])


def body(timeline, pointing, plate_angle, detector_angle, detector_weight, kernel, tile_owner, tile_block, wiener):
    taps = jnp.pad(kernel.astype(F32), (0, TAPS_ROW - kernel.shape[0])).reshape(1, TAPS_ROW)
    vmem = pl.BlockSpec(memory_space=pltpu.VMEM)
    dma = pltpu.SemaphoreType.DMA
    spectrum = pl.pallas_call(
        map_kernel,
        out_shape=jax.ShapeDtypeStruct((2, 3, 32, ROWS), F32),
        in_specs=[pl.BlockSpec(memory_space=pl.ANY)] * 9,
        out_specs=vmem,
        scratch_shapes=[
            pltpu.VMEM((ROWS, 256), F32),
            pltpu.VMEM((2, 8, 2, 256, 256), BF16),
            pltpu.VMEM((4, 128), F32),
            pltpu.VMEM((1, DET), F32),
            pltpu.VMEM((1, DET), F32),
            pltpu.VMEM((1, TAPS_ROW), F32),
            pltpu.VMEM((1, NTILE), jnp.int32),
            pltpu.VMEM((1, NTILE), jnp.int32),
            dma((10,)),
            pltpu.VMEM((3 * TS, DET), BF16),
            pltpu.VMEM((256, TAPS_PAD), BF16),
            pltpu.VMEM((2, TS, DET), F32),
            pltpu.VMEM((6, TS, 128), F32),
            pltpu.VMEM((2, TS, 128), jnp.int32),
            pltpu.VMEM((192, PIECE * DGRP), BF16),
            pltpu.VMEM((128, PIECE * DGRP), BF16),
            pltpu.VMEM((NTILE, 384), F32),
            pltpu.VMEM((2, SIDE, SIDE, NTILE, 384), BF16),
            pltpu.VMEM((8, 16, 1, 128), jnp.int32),
            pltpu.VMEM((768, 256), BF16),
            pltpu.VMEM((64, 256), BF16),
            dma((2,)), dma((2,)), dma((15,)), dma((15,)), dma((7,)), dma((7,)),
            dma((8,)), dma((8,)), dma((16,)), dma((16,)), dma((16,)), dma((16,)),
        ],
        compiler_params=pltpu.CompilerParams(
            collective_id=0, has_side_effects=True, vmem_limit_bytes=64 << 20
        ),
        cost_estimate=pl.CostEstimate(flops=20 << 30, bytes_accessed=4 << 20, transcendentals=1 << 20),
    )(
        timeline,
        pointing,
        plate_angle.reshape(4, 128),
        detector_angle.reshape(1, DET),
        detector_weight.reshape(1, DET),
        taps,
        tile_owner.reshape(1, NTILE),
        tile_block.reshape(1, NTILE),
        jnp.asarray(column_tables()),
    )
    return spectrum * wiener[None]


def solution(mesh):
    placed = (
        P("tm", "band"),
        P("tm", "band"),
        P("tm"),
        P("band"),
        P("band"),
        P("band"),
        P("tm", "band"),
        P("tm", "band"),
        P("band", "tm", None),
    )
    return jax.shard_map(
        body, mesh=mesh, in_specs=placed, out_specs=P(None, "band", "tm", None), check_vma=False
    )
```

```python
import functools
import math

import jax
import jax.numpy as jnp
import numpy as np
from jax import lax
from jax.experimental import pallas as pl
from jax.experimental.pallas import tpu as pltpu
from jax.sharding import PartitionSpec as P

DET = 256
TS = 512
PIECE = 16
DGRP = 128
BPIX = 128
ROWS = 2048
COLS = 4096
NTILE = 64
N_TM = 128
SIDE = 8
TAPS_PAD = 1280
TAPS_ROW = 2048
MESH = pl.DeviceIdType.MESH
F32 = jnp.float32
BF16 = jnp.bfloat16


def dot(a, b, dims=((1,), (0,))):
    return lax.dot_general(a, b, (dims, ((), ())), preferred_element_type=F32)


def iota(shape, axis):
    return lax.broadcasted_iota(jnp.int32, shape, axis)


def eighth(parts):
    def add(u, v):
        return (u[0] + v[0], u[1] + v[1])

    def sub(u, v):
        return (u[0] - v[0], u[1] - v[1])

    def turn(u):
        return (u[1], -u[0])

    def four(u):
        s, d, t, e = add(u[0], u[2]), sub(u[0], u[2]), add(u[1], u[3]), turn(sub(u[1], u[3]))
        return [add(s, t), add(d, e), sub(s, t), sub(d, e)]

    even, odd = four(parts[0::2]), four(parts[1::2])
    h = math.sqrt(0.5)
    odd[1] = ((odd[1][0] + odd[1][1]) * h, (odd[1][1] - odd[1][0]) * h)
    odd[2] = turn(odd[2])
    odd[3] = ((odd[3][1] - odd[3][0]) * h, (-odd[3][0] - odd[3][1]) * h)
    return [add(even[k], odd[k]) for k in range(4)] + [sub(even[k], odd[k]) for k in range(4)]


def finish_columns(rows, tables, out):
    lines = []
    for r in range(8):
        at = slice(r * 256, r * 256 + 256)
        both = jnp.concatenate(
            [jnp.transpose(rows[at, 0:128])[0:96], jnp.transpose(rows[at, 128:256])[0:96]], axis=0
        )
        upper = both.astype(BF16)
        stacked = jnp.concatenate([upper, (both - upper.astype(F32)).astype(BF16)], axis=0)
        waves = []
        for w in range(2):
            wide = dot(stacked, tables[0, r, w])
            waves.append(wide[0:192] + wide[192:384] + dot(upper, tables[1, r, w]))
        lines.append((waves[0][0:96] + waves[1][96:192], waves[0][96:192] - waves[1][0:96]))
    scale = 1.0 / math.sqrt(ROWS * COLS)
    for k, (real, imag) in enumerate(eighth(lines)):
        at = slice(k * 256, k * 256 + 256)
        for s in range(3):
            out[0, s, :, at] = real[s * 32 : s * 32 + 32] * scale
            out[1, s, :, at] = imag[s * 32 : s * 32 + 32] * scale


def map_kernel(
    timeline_in, pointing_in, plate_in, det_angle_in, det_weight_in, taps_in, owner_in, block_in,
    tables_in, out,
    rows, tables,
    plate, det_angle, det_weight, taps, owner, block, fetched,
    window, toep, trig, vals, pixels, spread, low_hot, local, gathered, meta, basis, turn,
    halo_send, halo_recv, m1_send, m1_recv, m2_send, m2_recv,
    p1_send, p1_recv, p2_send, p2_recv, sib_send, sib_recv,
):
    band = lax.axis_index("band")
    me = lax.axis_index("tm")
    y = me // 16
    z = (me // 2) % SIDE
    c = me % 2
    zc = me % 16

    def dev(yy, zz, cc):
        return (band, (yy % SIDE) * 16 + (zz % SIDE) * 2 + cc)

    def fetch(k, src, dst):
        copy = pltpu.make_async_copy(src, dst, fetched.at[k])
        copy.start()
        return copy

    own = window.at[pl.ds(TS, TS)]
    fetch_codes = [fetch(0, owner_in, owner), fetch(1, block_in, block)]
    fetch_samples = fetch(2, timeline_in, own)
    fetch_rest = [
        fetch(3, plate_in, plate),
        fetch(4, det_angle_in, det_angle),
        fetch(5, det_weight_in, det_weight),
        fetch(6, taps_in, taps),
    ]
    fetch_pixels = [
        fetch(7 + half, pointing_in.at[:, pl.ds(half * 128, 128)], pixels.at[half]) for half in range(2)
    ]

    right, left = (band, (me + 1) % N_TM), (band, (me + N_TM - 1) % N_TM)
    plane = [(band, y * 16 + (zc + k) % 16) for k in range(1, 16)]
    column = [dev(y + k, z, c) for k in range(1, SIDE)]
    barrier = pltpu.get_barrier_semaphore()
    for other in plane + column + [right, left]:
        pl.semaphore_signal(barrier, inc=1, device_id=other, device_id_type=MESH)

    for copy in fetch_codes:
        copy.wait()
    lane = iota((NTILE, 128), 1)
    q, a = (lane % NTILE) // 8, lane % 8
    wanted = ((q // 2) * 8 + a) * 2 + q % 2
    place = jnp.where((lane // NTILE == c) & (wanted == iota((NTILE, 128), 0)), 1.0, 0.0)
    sub = iota((8, NTILE), 0)
    parts = jnp.where(
        sub == 0, owner[...], jnp.where(sub == 1, block[...] // 32, block[...] % 32)
    ).astype(F32)
    spots = dot(parts.astype(BF16), place.astype(BF16)).astype(jnp.int32)
    meta[y, zc] = (spots[0:1] * 16 + spots[1:2]) * 32 + spots[2:3]

    fetch_samples.wait()
    pl.semaphore_wait(barrier, 24)

    def remote(src, dst, send, recv, to):
        copy = pltpu.make_async_remote_copy(
            src_ref=src, dst_ref=dst, send_sem=send, recv_sem=recv, device_id=to, device_id_type=MESH
        )
        copy.start()
        return copy

    pending = []
    halo = [
        remote(own, window.at[pl.ds(0, TS)], halo_send.at[0], halo_recv.at[0], right),
        remote(own, window.at[pl.ds(2 * TS, TS)], halo_send.at[1], halo_recv.at[1], left),
    ]
    first_meta = [
        remote(meta.at[y, zc], meta.at[y, zc], m1_send.at[k], m1_recv.at[k], to)
        for k, to in enumerate(plane)
    ]

    fetch_late = [fetch(9, tables_in, tables)]
    for copy in fetch_rest:
        copy.wait()
    band_rows = jnp.broadcast_to(taps[:, 0:TAPS_PAD], (256, TAPS_PAD))
    toep[...] = pltpu.roll(band_rows, 0, 1, stride=1, stride_axis=0).astype(BF16)
    plate_cos, plate_sin = jnp.cos(4.0 * plate[...]), jnp.sin(4.0 * plate[...])
    det_cos, det_sin = jnp.cos(2.0 * det_angle[...]), jnp.sin(2.0 * det_angle[...])
    for part in range(4):
        times = slice(part * 128, part * 128 + 128)
        cos_t = jnp.transpose(jnp.broadcast_to(plate_cos[part : part + 1], (128, 128)))
        sin_t = jnp.transpose(jnp.broadcast_to(plate_sin[part : part + 1], (128, 128)))
        for half in range(2):
            lanes = slice(half * 128, half * 128 + 128)
            trig[0, times, lanes] = cos_t * det_cos[:, lanes] - sin_t * det_sin[:, lanes]
            trig[1, times, lanes] = sin_t * det_cos[:, lanes] + cos_t * det_sin[:, lanes]

    rows[...] = jnp.zeros_like(rows)
    for copy in halo:
        copy.wait_recv()

    @pl.when(me == 0)
    def _():
        window[0:TS, :] = jnp.zeros((TS, DET), BF16)

    @pl.when(me == N_TM - 1)
    def _():
        window[2 * TS : 3 * TS, :] = jnp.zeros((TS, DET), BF16)

    for part in range(2):
        times = slice(part * 256, part * 256 + 256)
        filtered = dot(toep[...], window[part * 256 : part * 256 + TAPS_PAD, :])
        weighted = det_weight[...] * filtered
        for half in range(2):
            lanes = slice(half * 128, half * 128 + 128)
            vals[half, times, :] = weighted[:, lanes]
            vals[2 + half, times, :] = weighted[:, lanes] * trig[0, times, lanes]
            vals[4 + half, times, :] = weighted[:, lanes] * trig[1, times, lanes]

    for copy in fetch_pixels:
        copy.wait()
    lane = iota((8, 128), 1)
    pick = (lane // 8) * 8 + iota((8, 128), 0)

    def bin_tiles(q, carry):
        first = (q // 2) * 128
        for t in range(PIECE):
            where = pl.ds(first + t, 8, stride=PIECE)
            pixel = pixels[q % 2, where, :]
            high, low = pixel // 16, pixel % 16
            value = [vals[2 * s + q % 2, where, :] for s in range(3)]
            at = slice(t * 128, t * 128 + 128)
            for pair in range(12):
                both = []
                for k in (2 * pair, 2 * pair + 1):
                    both.append(jnp.where(high == k // 3, value[k % 3], 0.0))
                spread[pair * 16 : pair * 16 + 16, at] = jnp.concatenate(both, axis=0).astype(BF16)
            for pair in range(8):
                both = [jnp.where(low == k, 1.0, 0.0) for k in (2 * pair, 2 * pair + 1)]
                low_hot[pair * 16 : pair * 16 + 16, at] = jnp.concatenate(both, axis=0).astype(BF16)
        crossed = dot(spread[...], low_hot[...], ((1,), (1,)))
        for s in range(3):
            total = jnp.zeros((8, 128), F32)
            for h in range(8):
                k = h * 3 + s
                own = jnp.take_along_axis(crossed[k * 8 : k * 8 + 8], pick, axis=1)
                total = jnp.where(lane % 8 == h, own, total)
            local[pl.ds(pl.multiple_of(q * 8, 8), 8), s * 128 : s * 128 + 128] = total
        return carry

    lax.fori_loop(0, 8, bin_tiles, 0)

    pending += halo + first_meta

    c1, c0 = c, 1 - c
    up = dev(y + c0, z + c1, c)
    down = dev(y + SIDE - c0, z + SIDE - c1, c)
    peers = [dev(y + c1 * k, z + c0 * k, c) for k in range(1, SIDE)]
    sibling = dev(y, z, 1 - c)

    gathered[c, 0, 0] = local[...].astype(BF16)

    def carry(src, dst, send, recv, to):
        return pltpu.make_async_remote_copy(
            src_ref=src, dst_ref=dst, send_sem=send, recv_sem=recv, device_id=to, device_id_type=MESH
        )

    def four(d2, h):
        return gathered.at[c, d2, pl.ds(pl.multiple_of(h * 4, 4), 4)]

    def to_peer(k):
        src, dst = gathered.at[c, 0, 0], gathered.at[c, 0, k]
        return carry(src, dst, p1_send.at[k], p1_recv.at[k], peers[k - 1])

    def to_line(d2, h, step):
        to, then = up if step == 1 else down, (d2 + step) % SIDE
        at = then * 2 + h
        return carry(four(d2, h), four(then, h), p2_send.at[at], p2_recv.at[at], to)

    def to_sibling(d2, h):
        at = d2 * 2 + h
        return carry(four(d2, h), four(d2, h), sib_send.at[at], sib_recv.at[at], sibling)

    for k in (1, 2, 3, 7, 6, 5, 4):
        to_peer(k).start()
    for copy in first_meta:
        copy.wait_recv()
    second_meta = [
        remote(meta.at[y], meta.at[y], m2_send.at[k], m2_recv.at[k], to)
        for k, to in enumerate(column)
    ]
    pending += second_meta

    row = iota((BPIX, 128), 0)
    lane = iota((BPIX, 128), 1)
    pixel = (row % 8) * 16 + row // 8
    step = (((me * 32 + lane % 32) * pixel) % COLS).astype(F32) * (2.0 * math.pi / COLS)
    cos_x, sin_x = jnp.cos(step), jnp.sin(step)
    for s in range(3):
        mine = lane // 32 == s
        whole = jnp.concatenate([jnp.where(mine, cos_x, 0.0), jnp.where(mine, -sin_x, 0.0)], axis=1)
        high = whole.astype(BF16)
        basis[s * 128 : s * 128 + 128, :] = high
        basis[384 + s * 128 : 384 + s * 128 + 128, :] = (whole - high.astype(F32)).astype(BF16)
    step = ((iota((32, 128), 0) * (iota((32, 128), 1) % 32)) % 32).astype(F32) * (2.0 * math.pi / 32)
    whole = jnp.concatenate([jnp.cos(step), jnp.sin(step)], axis=1)
    high = whole.astype(BF16)
    turn[0:32, :] = high
    turn[32:64, :] = (whole - high.astype(F32)).astype(BF16)

    for h in range(2):
        for d1 in ((1, 2, 3), (7, 6, 5, 4))[h]:
            to_peer(d1).wait_recv()
        to_line(0, h, 1).start()
        to_line(0, h, 7).start()
        to_sibling(0, h).start()
    for copy in second_meta:
        copy.wait_recv()

    def arrive(d2, h, step):
        to_line((d2 + SIDE - step) % SIDE, h, step).wait_recv()

    def members(g):
        k = (g + 1) // 2
        single = (7 - g % 7) // 7
        for sign in range(2):
            yield (k + sign * (8 - 2 * k)) % SIDE, single * sign + (1 - single) * ((g + 1) % 2)

    key_rows = iota((256, 1024), 0).astype(F32).astype(BF16)
    turn_rows = iota((64, 1024), 0) % 32

    def each_group(g, state):
        k, h = 1 + g // 2, g % 2

        @pl.when(g < 6)
        def _():
            for step in (1, 7):
                d2 = k if step == 1 else SIDE - k
                arrive(d2, h, step)

                @pl.when(k < 3)
                def _():
                    to_line(d2, h, step).start()

                @pl.when((k == 3) & (h == (0 if step == 1 else 1)))
                def _():
                    to_line(d2, h, step).start()

                to_sibling(d2, h).start()

        @pl.when(g == 6)
        def _():
            for last in range(2):
                arrive(4, last, 1 if last == 0 else 7)
                to_sibling(4, last).start()

        tiles, codes = [], []
        for d2, quad in members(g):
            to_sibling(d2, quad).wait_recv()
            for i in range(4):
                d1 = quad * 4 + i
                tiles += [gathered[0, d2, d1], gathered[1, d2, d1]]
                far, near = (y + SIDE - d2) % SIDE, (z + SIDE - d1) % SIDE
                across, along = (y + SIDE - d1) % SIDE, (z + SIDE - d2) % SIDE
                codes.append(meta[far, near * 2] + meta[across, along * 2 + 1])
        tiles, codes = jnp.concatenate(tiles, axis=0), jnp.concatenate(codes, axis=1)
        spectra = dot(jnp.concatenate([tiles, tiles], axis=1), basis[...])
        turn_hot = jnp.where(turn_rows == codes % 32, 1.0, 0.0).astype(BF16)
        turned = dot(turn_hot, turn[...], ((0,), (0,)))
        real, imag = spectra[:, 0:128], spectra[:, 128:256]
        cos_b, sin_b = turned[:, 0:128], turned[:, 128:256]
        moved = jnp.concatenate(
            [real * cos_b + imag * sin_b, imag * cos_b - real * sin_b], axis=1
        ).astype(BF16)
        map_row = codes // 32
        low, high = map_row % 8, map_row // 8
        for r in range(8):
            key = jnp.where(low == r, high, -1).astype(F32).astype(BF16)
            hot = jnp.where(key_rows == key, jnp.bfloat16(1), jnp.bfloat16(0))
            rows[r * 256 : r * 256 + 256, :] += dot(hot, moved)
        return state

    lax.fori_loop(0, 8, each_group, 0)

    for copy in fetch_late:
        copy.wait()
    finish_columns(rows, tables, out)

    for copy in pending:
        copy.wait_send()
    for k in range(1, 8):
        to_peer(k).wait_send()

    def sent(n, state):
        d2, h = n // 2, n % 2
        to_sibling(d2, h).wait_send()

        @pl.when(d2 > 0)
        def _():
            to_line((d2 + SIDE - 1) % SIDE, h, 1).wait_send()

        return state

    lax.fori_loop(0, 16, sent, 0)


def column_tables():
    r0 = np.arange(256)[None, :, None]
    r1 = np.arange(8)[:, None, None]
    k = np.arange(256)[None, None, :]
    phase = (k * (r1 + 8 * r0) % ROWS) * (2.0 * np.pi / ROWS)
    table = np.stack([np.cos(phase), np.sin(phase)], axis=1)
    high = table.astype(BF16)
    low = (table - high.astype(np.float64)).astype(BF16)
    return np.stack([high, low])


def weigh(spectrum, wiener, out):
    out[...] = spectrum[...] * wiener[...][None]


def body(timeline, pointing, plate_angle, detector_angle, detector_weight, kernel, tile_owner, tile_block, wiener):
    taps = jnp.pad(kernel.astype(F32), (0, TAPS_ROW - kernel.shape[0])).reshape(1, TAPS_ROW)
    vmem = pl.BlockSpec(memory_space=pltpu.VMEM)
    dma = pltpu.SemaphoreType.DMA
    spectrum = pl.pallas_call(
        map_kernel,
        out_shape=jax.ShapeDtypeStruct((2, 3, 32, ROWS), F32),
        in_specs=[pl.BlockSpec(memory_space=pl.ANY)] * 9,
        out_specs=vmem,
        scratch_shapes=[
            pltpu.VMEM((ROWS, 256), F32),
            pltpu.VMEM((2, 8, 2, 256, 256), BF16),
            pltpu.VMEM((4, 128), F32),
            pltpu.VMEM((1, DET), F32),
            pltpu.VMEM((1, DET), F32),
            pltpu.VMEM((1, TAPS_ROW), F32),
            pltpu.VMEM((1, NTILE), jnp.int32),
            pltpu.VMEM((1, NTILE), jnp.int32),
            dma((10,)),
            pltpu.VMEM((3 * TS, DET), BF16),
            pltpu.VMEM((256, TAPS_PAD), BF16),
            pltpu.VMEM((2, TS, DET), F32),
            pltpu.VMEM((6, TS, 128), F32),
            pltpu.VMEM((2, TS, 128), jnp.int32),
            pltpu.VMEM((192, PIECE * DGRP), BF16),
            pltpu.VMEM((128, PIECE * DGRP), BF16),
            pltpu.VMEM((NTILE, 384), F32),
            pltpu.VMEM((2, SIDE, SIDE, NTILE, 384), BF16),
            pltpu.VMEM((8, 16, 1, 128), jnp.int32),
            pltpu.VMEM((768, 256), BF16),
            pltpu.VMEM((64, 256), BF16),
            dma((2,)), dma((2,)), dma((15,)), dma((15,)), dma((7,)), dma((7,)),
            dma((8,)), dma((8,)), dma((16,)), dma((16,)), dma((16,)), dma((16,)),
        ],
        compiler_params=pltpu.CompilerParams(
            collective_id=0, has_side_effects=True, vmem_limit_bytes=64 << 20
        ),
        cost_estimate=pl.CostEstimate(flops=20 << 30, bytes_accessed=4 << 20, transcendentals=1 << 20),
    )(
        timeline,
        pointing,
        plate_angle.reshape(4, 128),
        detector_angle.reshape(1, DET),
        detector_weight.reshape(1, DET),
        taps,
        tile_owner.reshape(1, NTILE),
        tile_block.reshape(1, NTILE),
        jnp.asarray(column_tables()),
    )
    both = pl.BlockSpec((2, 1, 32, ROWS), lambda s: (0, s, 0, 0))
    return pl.pallas_call(
        weigh,
        grid=(3,),
        out_shape=jax.ShapeDtypeStruct((2, 3, 32, ROWS), F32),
        in_specs=[both, pl.BlockSpec((1, 32, ROWS), lambda s: (s, 0, 0))],
        out_specs=both,
        compiler_params=pltpu.CompilerParams(vmem_limit_bytes=64 << 20),
    )(spectrum, wiener)


def solution(mesh):
    placed = (
        P("tm", "band"),
        P("tm", "band"),
        P("tm"),
        P("band"),
        P("band"),
        P("band"),
        P("tm", "band"),
        P("tm", "band"),
        P("band", "tm", None),
    )
    return jax.shard_map(
        body, mesh=mesh, in_specs=placed, out_specs=P(None, "band", "tm", None), check_vma=False
    )
```
